768 devices in a mesh: mp: 96 (over x, z, y_lo), station: 8 (over y_hi, core).
Axes of the slice: x: 4, y: 8 (y_hi: 4, y_lo: 2; y = y_hi * 2 + y_lo), z: 12, core: 2. Of those that a mesh axis runs over, the one named last changes fastest.
Arguments:
- p_now: float32 [768, 64, 128], P('mp'), may hold values from -2.7 to 2.7
- p_prev: float32 [768, 64, 128], P('mp'), may hold values from -2.7 to 2.7
- velocity: float32 [768, 64, 128], P('mp'), may hold values from 4 to 4.5
- density: float32 [768, 64, 128], P('mp'), may hold values from -6 to 6
- wavelet: float32 [16], replicated, may hold values from -4 to 4
- source_cell: int32 [1], replicated, may hold values from 0 to 6291455
- receiver_cells: int32 [256], replicated, may hold values from 0 to 49151
- station_cells: int32 [1024], P('station'), may hold values from 0 to 49151
- observed: float32 [1024], P('station'), may hold values from -6 to 6
Outputs:
- wavefield: float32 [768, 64, 128], P('mp')
- traces: float32 [16, 256], replicated
- gravity_residual: float32 [1024], P('station')
- density_gradient: float32 [768, 64, 128], P('mp', 'station')
- cross_gradient: float32 [3, 768, 64, 128], P(None, 'mp')
The draws below stay inside these ranges and needn't reach their ends.
All inputs are finite; a program needn't handle non-finite values.
Results may differ from the reference program's by a relative error of at most 0.0036.
The reference program's roundings to bfloat16 on the way count: a program that leaves them out, or rounds other values in their place, can miss the bound.
Values sent between devices are 32-bit elements; how exact they have to be, the bound alone decides.
A program may use at most 32 MiB of HBM per device.

```python
import math
import jax
import jax.numpy as jnp
from jax import lax

NY = 64
NZ = 128
NREC = 256
STEPS = 16
NX = 768
STATIONS = 1024


def draw_density(key, part):
    values = jax.random.normal(key, (NX, NY, NZ), jnp.float32)
    values = jnp.clip(values, -6.0, 6.0)
    return values


def pressure_pair(key):
    amp_key = jax.random.fold_in(key, 11)
    ratio_key = jax.random.fold_in(key, 23)
    parity = (jnp.arange(NX, dtype=jnp.int32)[:, None, None] + jnp.arange(NY, dtype=jnp.int32)[None, :, None] + jnp.arange(NZ, dtype=jnp.int32)[None, None, :]) % 2
    signs = 1.0 - 2.0 * parity.astype(jnp.float32)
    amplitude = jnp.clip(1.5 + 0.6 * jax.random.normal(amp_key, (NX, NY, NZ), jnp.float32), 0.3, 2.7)
    ratio = jax.random.uniform(ratio_key, (NX, NY, NZ), jnp.float32, 0.6, 1.0)
    now_values = signs * amplitude
    prev_values = -now_values * ratio
    return (now_values, prev_values)


def draw_p_now(key, part):
    now_values, prev_values = pressure_pair(key)
    return now_values


def draw_p_prev(key, part):
    now_values, prev_values = pressure_pair(key)
    return prev_values


def touch_ends(drawn, key, smallest, top_value):
    index_at = [jax.random.randint(jax.random.fold_in(key, axis), (), 0, length) for axis, length in enumerate(drawn.shape)]
    widest = drawn.shape.index(max(drawn.shape))
    beside = index_at[:widest] + [(index_at[widest] + 1) % drawn.shape[widest]] + index_at[widest + 1:]
    return drawn.at[tuple(index_at)].set(smallest).at[tuple(beside)].set(top_value)


def level_of(key, extent, pieces, low, top_value):
    def one(dim, blocks):
        steps = jax.random.uniform(jax.random.fold_in(jax.random.fold_in(key, 6), dim), (blocks,), jnp.float32, low / len(pieces), top_value / len(pieces))
        return jnp.repeat(jnp.exp(steps), extent[dim] // blocks).reshape((-1,) + (1,) * (len(extent) - dim - 1))

    factor_of = one(*pieces[0])
    for cut in pieces[1:]:
        factor_of = factor_of * one(*cut)
    return factor_of


def centred(stream_key, shape, scale, limit, split=(), kind=jnp.bfloat16):
    values = scale * jax.random.normal(stream_key, shape, jnp.float32)
    if split:
        values = values * level_of(stream_key, shape, split, -0.22, 0.18)
    return jnp.clip(values, -limit, limit).astype(kind)


def setup_inputs(seed: int = 0) -> dict:
    key_of = jax.random.split(jax.random.key(seed), 10)
    p_now = draw_p_now(jax.random.fold_in(key_of[9], 71), 0)
    p_prev = draw_p_prev(jax.random.fold_in(key_of[9], 71), 0)
    velocity = jnp.clip(jnp.exp(math.log(4.5) - 0.117783036 * jax.random.uniform(key_of[2], (NX, NY, NZ), jnp.float32) ** level_of(key_of[2], (NX, NY, NZ), ((0, 96),), -0.2, 0.2)), 4.0, 4.5)
    density = draw_density(jax.random.fold_in(key_of[9], 71), 0)
    wavelet = centred(key_of[4], (STEPS,), 1.0, 4.0, (), jnp.float32)
    source_cell = jax.random.randint(key_of[5], (1,), 0, NX * NY * NZ).astype(jnp.int32)
    receiver_cells = touch_ends(jax.random.randint(key_of[6], (NREC,), 0, NX * NY), jax.random.fold_in(key_of[6], 1), 0, (NX * NY) - 1).astype(jnp.int32)
    station_cells = touch_ends(jax.random.randint(key_of[7], (STATIONS,), 0, NX * NY), jax.random.fold_in(key_of[7], 1), 0, (NX * NY) - 1).astype(jnp.int32)
    observed = centred(key_of[8], (STATIONS,), 1.0, 6.0, ((0, 8),), jnp.float32)
    return {"p_now": p_now, "p_prev": p_prev, "velocity": velocity, "density": density, "wavelet": wavelet, "source_cell": source_cell, "receiver_cells": receiver_cells, "station_cells": station_cells, "observed": observed}


STENCIL = (-205.0 / 72.0, 8.0 / 5.0, -1.0 / 5.0, 8.0 / 315.0, -1.0 / 560.0)
TIME_RATIO = 0.1

def stencil(padded, current):
    slab, lateral, vertical = current.shape
    result = 3.0 * STENCIL[0] * current
    for distance in range(1, 5):
        pairs = padded[4 + distance:4 + distance + slab, 4:4 + lateral, 4:4 + vertical]
        pairs = pairs + padded[4 - distance:4 - distance + slab, 4:4 + lateral, 4:4 + vertical]
        pairs = pairs + padded[4:4 + slab, 4 + distance:4 + distance + lateral, 4:4 + vertical]
        pairs = pairs + padded[4:4 + slab, 4 - distance:4 - distance + lateral, 4:4 + vertical]
        pairs = pairs + padded[4:4 + slab, 4:4 + lateral, 4 + distance:4 + distance + vertical]
        pairs = pairs + padded[4:4 + slab, 4:4 + lateral, 4 - distance:4 - distance + vertical]
        result = result + STENCIL[distance] * pairs
    return result

def kernel_tile(plane_x, station_x, station_y, cell_y, cell_z):
    delta_x = plane_x - station_x
    delta_y = cell_y[None, :] - station_y[:, None]
    radius_sq = delta_x[:, None] * delta_x[:, None] + delta_y * delta_y + cell_z[None, :] * cell_z[None, :]
    return (cell_z[None, :] / (radius_sq * jnp.sqrt(radius_sq))).astype(jnp.bfloat16)

def cross_terms(padded, slab, lateral, vertical):
    diff_x = (padded[:, 2:2 + slab, 1:1 + lateral, 1:1 + vertical] - padded[:, 0:slab, 1:1 + lateral, 1:1 + vertical]) * 0.5
    diff_y = (padded[:, 1:1 + slab, 2:2 + lateral, 1:1 + vertical] - padded[:, 1:1 + slab, 0:lateral, 1:1 + vertical]) * 0.5
    diff_z = (padded[:, 1:1 + slab, 1:1 + lateral, 2:2 + vertical] - padded[:, 1:1 + slab, 1:1 + lateral, 0:vertical]) * 0.5
    first = diff_y[0] * diff_z[1] - diff_z[0] * diff_y[1]
    second = diff_z[0] * diff_x[1] - diff_x[0] * diff_z[1]
    third = diff_x[0] * diff_y[1] - diff_y[0] * diff_x[1]
    return jnp.stack([first, second, third])

def reference(p_now, p_prev, velocity, density, wavelet, source_cell, receiver_cells, station_cells, observed):
    courant = TIME_RATIO * velocity * (TIME_RATIO * velocity)
    flat_index = (jnp.arange(NX, dtype=jnp.int32)[:, None, None] * NY + jnp.arange(NY, dtype=jnp.int32)[None, :, None]) * NZ + jnp.arange(NZ, dtype=jnp.int32)[None, None, :]
    source_mask = (flat_index == source_cell[0]).astype(jnp.float32)

    def advance(carry, pulse):
        current, previous = carry
        padded = jnp.pad(current, 4)
        updated = 2.0 * current - previous + courant * stencil(padded, current) + pulse * source_mask
        surface = updated[:, :, 0].reshape(-1)
        return ((updated, current), surface[receiver_cells])
    (wavefield, unused), traces = lax.scan(advance, (p_now, p_prev), wavelet)
    station_x = (station_cells // NY).astype(jnp.float32)
    station_y = (station_cells % NY).astype(jnp.float32)
    cell_y = (jnp.arange(NY * NZ, dtype=jnp.int32) // NZ).astype(jnp.float32)
    cell_z = (jnp.arange(NY * NZ, dtype=jnp.int32) % NZ).astype(jnp.float32) + 1.0
    planes = density.astype(jnp.bfloat16).reshape(NX, NY * NZ)
    plane_xs = jnp.arange(NX, dtype=jnp.int32).astype(jnp.float32)

    def forward(totals, packed):
        plane_x, plane = packed
        tile = kernel_tile(plane_x, station_x, station_y, cell_y, cell_z)
        return (totals + jnp.dot(tile, plane, preferred_element_type=jnp.float32), None)
    predicted, unused_out = lax.scan(forward, jnp.zeros((STATIONS,), jnp.float32), (plane_xs, planes))
    gravity_residual = predicted - observed
    residual_low = gravity_residual.astype(jnp.bfloat16)

    def adjoint(plane_x):
        tile = kernel_tile(plane_x, station_x, station_y, cell_y, cell_z)
        return jnp.dot(residual_low, tile, preferred_element_type=jnp.float32)
    density_gradient = lax.map(adjoint, plane_xs).reshape(NX, NY, NZ)
    stacked = jnp.stack([velocity, density])
    padded_model = jnp.pad(stacked, ((0, 0), (1, 1), (1, 1), (1, 1)))
    cross_gradient = cross_terms(padded_model, NX, NY, NZ)
    return (wavefield, traces, gravity_residual, density_gradient, cross_gradient)
```

```python
import functools

import jax
import jax.numpy as jnp
from jax import lax
from jax.experimental import pallas as pl
from jax.experimental.pallas import tpu as pltpu
from jax.sharding import Mesh
from jax.sharding import PartitionSpec as P

MP = ("x", "z", "y_lo")
STATION = ("station_hi", "core")
MESH = MP + STATION


STENCIL = (-205.0 / 72.0, 8.0 / 5.0, -1.0 / 5.0, 8.0 / 315.0, -1.0 / 560.0)
TIME_RATIO = 0.1
SPLIT = (4, 12, 2)


def extended(cells, sides, width):
    for axis, dim in sides:
        count = lax.axis_size(axis)
        ends = count - 1
        head = lax.slice_in_dim(cells, 0, width, axis=dim)
        tail = lax.slice_in_dim(cells, cells.shape[dim] - width, cells.shape[dim], axis=dim)
        cells = jnp.concatenate(
            [
                lax.ppermute(tail, axis, [(i, (i + 1) % count) for i in range(ends)]),
                cells,
                lax.ppermute(head, axis, [((i + 1) % count, i) for i in range(ends)]),
            ],
            axis=dim,
        )
    return cells


def over_axes(x, axes):
    for axis in axes:
        x = lax.psum(x, axis)
    return x


def turned_gather(arrays, axis, dims):
    turned = [jnp.moveaxis(a, dim, 0) for a, dim in zip(arrays, dims)]
    widths = [t[0].size for t in turned]
    both = jnp.concatenate([t.reshape(-1, w) for t, w in zip(turned, widths)], axis=1)
    result = lax.all_gather(both, axis, axis=0, tiled=True)
    blocks = jnp.split(result, [sum(widths[:k]) for k in range(1, len(widths))], axis=1)
    return tuple(
        (
            jnp.moveaxis(b.reshape(-1, *t.shape[1:]), 0, dim)
            for b, t, dim in zip(blocks, turned, dims)
        )
    )


MESH_ID = pl.DeviceIdType.MESH
SIDES = ((-1, 0), (1, 0), (0, -1), (0, 1), (-1, -1), (-1, 1), (1, -1), (1, 1))
ROW0 = 16
PLANE0 = 8


def place():
    x, z, low, high, core = (lax.axis_index(axis) for axis in MESH)
    nz = lax.axis_size("z")
    slab = (x * nz + z) * 2 + core
    return slab, high * 2 + low, low, core


def device_at(slab, block):
    nz = lax.axis_size("z")
    column = slab // 2
    return (column // nz, lax.rem(column, nz), lax.rem(block, 2), block // 2, lax.rem(slab, 2))


def advance(ref, prev, courant, mask, pulse, zmask, p0, planes, r0):
    rows = pl.ds(r0, 8)
    here = ref[pl.ds(p0, planes), rows, :]
    lap = 3.0 * STENCIL[0] * here
    for d in range(1, 5):
        pairs = ref[pl.ds(p0 + d, planes), rows, :] + ref[pl.ds(p0 - d, planes), rows, :]
        pairs = pairs + ref[pl.ds(p0, planes), pl.ds(r0 + d, 8), :]
        pairs = pairs + ref[pl.ds(p0, planes), pl.ds(r0 - d, 8), :]
        lap = lap + STENCIL[d] * pairs
        lap = lap + pltpu.roll(here, d, 2) * zmask[2 * d - 2][None]
        lap = lap + pltpu.roll(here, here.shape[2] - d, 2) * zmask[2 * d - 1][None]
    at = (pl.ds(p0, planes), rows)
    return 2.0 * here - prev[at] + courant[at] * lap + pulse * mask[at]


def wave_kernel(
    p_now, p_prev, velocity, wavelet, source, receivers, field, traces,
    w, v, courant, mask, zmask, hits,
    init_send, init_recv, halo_send, halo_recv, tail_send, tail_recv,
):
    slab, block, low, core = place()
    slabs = lax.axis_size(MP)
    blocks = lax.axis_size("station_hi") * 2
    lateral, vertical = p_now.shape[1:]
    same = core == low
    inner = 1 - 2 * core
    outer = -inner
    pair = 1 - 2 * low

    def there(ds, db):
        return (slab + ds >= 0) & (slab + ds < slabs) & (block + db >= 0) & (block + db < blocks)

    def window(b):
        start = jnp.clip(8 * (b - 1), 0, lateral - 24)
        return pl.multiple_of(start, 8), pl.multiple_of(ROW0 + start - 8 * b, 8)

    zero = jnp.zeros((24, 24, vertical), jnp.float32)
    for ref in (w.at[0], w.at[1], v, courant):
        ref[:, pl.ds(8, 24), :] = zero

    barrier = pltpu.get_barrier_semaphore()
    for other in range(2 * blocks):
        b, k = other // 2, other % 2

        @pl.when((b != block) | (k != core))
        def _():
            pl.semaphore_signal(
                barrier, 1, device_id=device_at(slab - core + k, b), device_id_type=MESH_ID
            )

    for db in (-1, 0, 1):

        @pl.when(there(outer, db))
        def _():
            pl.semaphore_signal(
                barrier, 1, device_id=device_at(slab + outer, block + db), device_id_type=MESH_ID
            )

    crossing = sum(jnp.where(there(outer, db), 1, 0) for db in (-1, 0, 1))
    pl.semaphore_wait(barrier, 2 * blocks - 1 + crossing)

    arrays = (p_now, p_prev, velocity)
    places = (w.at[0], v, courant)

    def own_package(b, target, k):
        start, to = window(b)
        return [
            pltpu.make_async_remote_copy(
                a.at[:, pl.ds(start, 24), :],
                p.at[pl.ds(PLANE0, 8), pl.ds(to, 24), :],
                init_send.at[k, n], init_recv.at[0, n], device_id=target, device_id_type=MESH_ID,
            )
            for n, (a, p) in enumerate(zip(arrays, places))
        ]

    def halo_package(b, side, target, k, landing):
        start, to = window(b)
        left = side < 0
        near_from = jnp.where(left, 4, 0)
        near_to = jnp.where(left, 4, 16)
        rows = pl.multiple_of(8 * b, 8)
        copies = [
            pltpu.make_async_remote_copy(
                p_now.at[:, pl.ds(start, 24), :],
                w.at[0, pl.ds(jnp.where(left, 0, 16), 8), pl.ds(to, 24), :],
                init_send.at[k, 0], init_recv.at[landing, 0],
                device_id=target, device_id_type=MESH_ID,
            )
        ]
        for n in (1, 2):
            copies.append(
                pltpu.make_async_remote_copy(
                    arrays[n].at[pl.ds(near_from, 4), pl.ds(rows, 8), :],
                    places[n].at[pl.ds(near_to, 4), pl.ds(ROW0, 8), :],
                    init_send.at[k, n], init_recv.at[landing, n],
                    device_id=target, device_id_type=MESH_ID,
                )
            )
        return copies

    paired = block + pair
    partner = device_at(slab, paired)

    @pl.when(same)
    def _():
        for copy in own_package(paired, partner, 0):
            copy.start()
        for k, b in ((1, block), (2, paired)):

            @pl.when(there(outer, 0))
            def _():
                for copy in halo_package(b, -outer, device_at(slab + outer, b), k, 2):
                    copy.start()

    @pl.when(jnp.logical_not(same))
    def _():
        for copy in halo_package(paired, inner, partner, 0, 1):
            copy.start()

    start, to = window(block)
    rows = pl.multiple_of(8 * block, 8)

    @pl.when(same)
    def _():
        for a, p in zip(arrays, places):
            p[pl.ds(PLANE0, 8), pl.ds(to, 24), :] = a[:, pl.ds(start, 24), :]

    @pl.when(jnp.logical_not(same))
    def _():
        left = inner < 0
        w[0, pl.ds(jnp.where(left, 0, 16), 8), pl.ds(to, 24), :] = p_now[:, pl.ds(start, 24), :]
        for a, p in ((p_prev, v), (velocity, courant)):
            p[pl.ds(jnp.where(left, 4, 16), 4), pl.ds(ROW0, 8), :] = a[
                pl.ds(jnp.where(left, 4, 0), 4), pl.ds(rows, 8), :
            ]

    source_cell = source[0]
    source_z = lax.rem(source_cell, vertical)
    source_xy = source_cell // vertical
    source_y = lax.rem(source_xy, lateral)
    source_x = source_xy // lateral
    shape = (24, 24, vertical)
    at_x = lax.broadcasted_iota(jnp.int32, shape, 0) + (8 * slab - PLANE0)
    at_y = lax.broadcasted_iota(jnp.int32, shape, 1) + (8 * block + 8 - ROW0)
    at_z = lax.broadcasted_iota(jnp.int32, shape, 2)
    hit = (at_x == source_x) & (at_y == source_y) & (at_z == source_z)
    mask[:, pl.ds(8, 24), :] = jnp.where(hit, 1.0, 0.0)
    lane = lax.broadcasted_iota(jnp.int32, (8, vertical), 1)
    for d in range(1, 5):
        zmask[2 * d - 2] = jnp.where(lane >= d, STENCIL[d], 0.0)
        zmask[2 * d - 1] = jnp.where(lane < vertical - d, STENCIL[d], 0.0)
    nrec = receivers.shape[1]
    cell = (8 * slab + lax.broadcasted_iota(jnp.int32, (8, 8, nrec), 0)) * lateral + (
        8 * block + lax.broadcasted_iota(jnp.int32, (8, 8, nrec), 1)
    )
    hits[...] = jnp.where(cell == receivers[...][None], 1.0, 0.0)

    @pl.when(same)
    def _():
        for copy in own_package(paired, partner, 0):
            copy.wait_send()
        for k, b in ((1, block), (2, paired)):

            @pl.when(there(outer, 0))
            def _():
                for copy in halo_package(b, -outer, device_at(slab + outer, b), k, 2):
                    copy.wait_send()

        for copy in halo_package(block, inner, partner, 0, 1):
            copy.wait_recv()

    @pl.when(jnp.logical_not(same))
    def _():
        for copy in halo_package(paired, inner, partner, 0, 1):
            copy.wait_send()
        for copy in own_package(block, partner, 0):
            copy.wait_recv()

    @pl.when(there(outer, 0))
    def _():
        for copy in halo_package(block, outer, partner, 0, 2):
            copy.wait_recv()

    scaled = TIME_RATIO * courant[:, pl.ds(8, 24), :]
    courant[:, pl.ds(8, 24), :] = scaled * scaled

    def region(ds, db, near):
        plane = PLANE0 + 8 * ds
        count = 8
        if near and ds:
            plane, count = (4, 4) if ds < 0 else (16, 4)
        return pl.ds(plane, count), pl.ds(ROW0 + 8 * db, 8)

    def halo(slot, k):
        ds, db = SIDES[k]
        corner = ds != 0 and db != 0
        to = region(-ds, -db, corner)
        if corner:
            begin = (PLANE0, ROW0)[0] + (4 if ds > 0 else 0)
            source_at = (pl.ds(begin, 4), pl.ds(ROW0, 8))
        else:
            source_at = (pl.ds(PLANE0, 8), pl.ds(ROW0, 8))
        opposite = SIDES.index((-ds, -db))
        return pltpu.make_async_remote_copy(
            w.at[(slot, *source_at)], w.at[(slot, *to)],
            halo_send.at[k], halo_recv.at[slot, opposite],
            device_id=device_at(slab + ds, block + db), device_id_type=MESH_ID,
        )

    def arriving(slot, k):
        ds, db = SIDES[k]
        corner = ds != 0 and db != 0
        at = region(ds, db, corner)
        return pltpu.make_async_remote_copy(
            w.at[(slot, *at)], w.at[(slot, *at)],
            halo_send.at[k], halo_recv.at[slot, k],
            device_id=device_at(slab + ds, block + db), device_id_type=MESH_ID,
        )

    own = (pl.ds(PLANE0, 8), pl.ds(ROW0, 8))

    def record(values, n):
        top = jnp.broadcast_to(values[:, :, 0:1], values.shape)
        for half in range(nrec // 128):
            part = jnp.sum(top * hits[:, :, half * 128 : (half + 1) * 128], axis=0)
            row = n * (nrec // 128) + half
            traces[pl.ds(row, 1), :] = jnp.sum(part, axis=0, keepdims=True)

    def first(slot, m):
        pulse = wavelet[2 * m]
        here = w.at[slot]
        for p0 in (4, 16):
            new = advance(here, v, courant, mask, pulse, zmask, p0, 4, ROW0)
            v[pl.ds(p0, 4), pl.ds(ROW0, 8), :] = new
        for p0 in range(8, 16, 2):
            for r0 in (12, 20):
                new = advance(here, v, courant, mask, pulse, zmask, p0, 2, r0)
                v[pl.ds(p0, 2), pl.ds(r0, 8), :] = new

    def second(slot, m, target):
        pulse = wavelet[2 * m + 1]
        for p0 in range(8, 16, 2):
            new = advance(v, w.at[slot], courant, mask, pulse, zmask, p0, 2, ROW0)
            target[pl.ds(p0, 2), pl.ds(ROW0, 8), :] = new

    pairs = wavelet.shape[0] // 2

    def body(m, unused):
        slot = lax.rem(m, 2)
        later = 1 - slot
        first(slot, m)
        second(slot, m, w.at[later])
        for k, (ds, db) in enumerate(SIDES):

            @pl.when(there(ds, db))
            def _():
                halo(later, k).start()

        record(v[own], 2 * m)
        record(w[(later, *own)], 2 * m + 1)
        for k, (ds, db) in enumerate(SIDES):

            @pl.when(there(ds, db))
            def _():
                halo(later, k).wait_send()
                arriving(later, k).wait_recv()

        return unused

    lax.fori_loop(0, pairs - 1, body, 0)
    slot = (pairs - 1) % 2
    first(slot, pairs - 1)
    second(slot, pairs - 1, w.at[1 - slot])
    last = w.at[1 - slot]

    def handing(high, k):
        return pltpu.make_async_remote_copy(
            last.at[own], field.at[:, pl.ds(rows, 8), :],
            tail_send.at[high, k], tail_recv.at[block],
            device_id=(*device_at(slab, 2 * high + core)[:4], k), device_id_type=MESH_ID,
        )

    for high in range(blocks // 2):
        for k in range(2):

            @pl.when((2 * high + core != block) | (k != core))
            def _():
                handing(high, k).start()

    @pl.when(same)
    def _():
        field[:, pl.ds(rows, 8), :] = last[own]

    record(v[own], 2 * pairs - 2)
    record(last[own], 2 * pairs - 1)
    for high in range(blocks // 2):
        for k in range(2):

            @pl.when((2 * high + core != block) | (k != core))
            def _():
                handing(high, k).wait_send()

    for b in range(blocks):

        @pl.when((b != block) | jnp.logical_not(same))
        def _():
            pltpu.make_async_remote_copy(
                last.at[own], field.at[:, pl.ds(8 * b, 8), :],
                tail_send.at[0, 0], tail_recv.at[b],
                device_id=partner, device_id_type=MESH_ID,
            ).wait_recv()


def wave(p_now, p_prev, velocity, wavelet, source_cell, receiver_cells):
    vertical = p_now.shape[2]
    nrec = receiver_cells.shape[0]
    blocks = lax.axis_size("station_hi") * 2
    f32 = jnp.float32
    padded = (24, 40, vertical)
    vmem, smem = (pl.BlockSpec(memory_space=space) for space in (pltpu.VMEM, pltpu.SMEM))
    dma = pltpu.SemaphoreType.DMA
    return pl.pallas_call(
        wave_kernel,
        out_shape=(
            jax.ShapeDtypeStruct(p_now.shape, f32),
            jax.ShapeDtypeStruct((wavelet.shape[0] * nrec // 128, 128), f32),
        ),
        in_specs=[vmem, vmem, vmem, smem, smem, vmem],
        out_specs=(vmem, vmem),
        scratch_shapes=[
            pltpu.VMEM((2, *padded), f32),
            pltpu.VMEM(padded, f32),
            pltpu.VMEM(padded, f32),
            pltpu.VMEM(padded, f32),
            pltpu.VMEM((8, 8, vertical), f32),
            pltpu.VMEM((8, 8, nrec), f32),
            dma((3, 3)), dma((3, 3)), dma((8,)), dma((2, 8)), dma((blocks // 2, 2)), dma((blocks,)),
        ],
        compiler_params=pltpu.CompilerParams(
            collective_id=0, has_side_effects=True, vmem_limit_bytes=32 * 2**20
        ),
    )(p_now, p_prev, velocity, wavelet, source_cell, receiver_cells.reshape(1, -1))


def kernel_tile(plane_x, station_x, station_y, cell_y, cell_z):
    delta_x = plane_x - station_x
    delta_y = cell_y[None, :] - station_y[:, None]
    radius_sq = (
        delta_x[:, None] * delta_x[:, None] + delta_y * delta_y + cell_z[None, :] * cell_z[None, :]
    )
    return (cell_z[None, :] / (radius_sq * jnp.sqrt(radius_sq))).astype(jnp.bfloat16)


def cross_terms(padded, slab, lateral, vertical):
    diff_x = (
        padded[:, 2 : 2 + slab, 1 : 1 + lateral, 1 : 1 + vertical]
        - padded[:, 0:slab, 1 : 1 + lateral, 1 : 1 + vertical]
    ) * 0.5
    diff_y = (
        padded[:, 1 : 1 + slab, 2 : 2 + lateral, 1 : 1 + vertical]
        - padded[:, 1 : 1 + slab, 0:lateral, 1 : 1 + vertical]
    ) * 0.5
    diff_z = (
        padded[:, 1 : 1 + slab, 1 : 1 + lateral, 2 : 2 + vertical]
        - padded[:, 1 : 1 + slab, 1 : 1 + lateral, 0:vertical]
    ) * 0.5
    first = diff_y[0] * diff_z[1] - diff_z[0] * diff_y[1]
    second = diff_z[0] * diff_x[1] - diff_x[0] * diff_z[1]
    third = diff_x[0] * diff_y[1] - diff_y[0] * diff_x[1]
    return jnp.stack([first, second, third])


def per_device(
    p_now, p_prev, velocity, density, wavelet, source_cell, receiver_cells, station_cells, observed
):
    slab, lateral, vertical = p_now.shape
    offset_x = lax.axis_index(MP) * slab
    offset_y = 0
    global_x = offset_x + jnp.arange(slab, dtype=jnp.int32)
    global_y = offset_y + jnp.arange(lateral, dtype=jnp.int32)
    last_field, traces = wave(p_now, p_prev, velocity, wavelet, source_cell, receiver_cells)
    traces = lax.psum(traces, MESH).reshape(-1, receiver_cells.shape[0])
    stacked = jnp.stack([velocity, density])
    padded_model = extended(stacked, ((MP, 1),), 1)
    padded_model = jnp.pad(padded_model, ((0, 0), (0, 0), (1, 1), (1, 1)))
    cross_gradient = cross_terms(padded_model, slab, lateral, vertical)
    station_x = (station_cells // lateral).astype(jnp.float32)
    station_y = (station_cells % lateral).astype(jnp.float32)
    cell_y = (jnp.arange(lateral * vertical, dtype=jnp.int32) // vertical).astype(jnp.float32)
    cell_z = (jnp.arange(lateral * vertical, dtype=jnp.int32) % vertical).astype(jnp.float32) + 1.0
    planes = density.astype(jnp.bfloat16).reshape(slab, lateral * vertical)
    plane_xs = global_x.astype(jnp.float32)

    def forward(totals, packed):
        plane_x, plane = packed
        tile = kernel_tile(plane_x, station_x, station_y, cell_y, cell_z)
        return (totals + jnp.dot(tile, plane, preferred_element_type=jnp.float32), None)

    partial_value, unused_out = lax.scan(
        forward, jnp.zeros((station_cells.shape[0],), jnp.float32), (plane_xs, planes)
    )
    predicted = over_axes(partial_value, MP)
    gravity_residual = predicted - observed
    share_rows = lateral // lax.axis_size(STATION)
    every_residual, every_x, every_y = turned_gather(
        (gravity_residual, station_x, station_y), STATION, (0, 0, 0)
    )
    every_low = every_residual.astype(jnp.bfloat16)
    share_index = jnp.arange(share_rows * vertical, dtype=jnp.int32)
    share_y = (lax.axis_index(STATION) * share_rows + share_index // vertical).astype(jnp.float32)
    share_z = (share_index % vertical).astype(jnp.float32) + 1.0

    def adjoint_rows(plane_x):
        tile = kernel_tile(plane_x, every_x, every_y, share_y, share_z)
        return jnp.dot(every_low, tile, preferred_element_type=jnp.float32)

    density_gradient = lax.map(adjoint_rows, plane_xs).reshape(slab, share_rows, vertical)
    return (last_field, traces, gravity_residual, density_gradient, cross_gradient)


def solution(mesh):
    split = Mesh(
        mesh.devices.reshape(*SPLIT, mesh.shape["station"] // 2, 2), MESH
    )
    slabs = P(MP, None, None)
    return jax.shard_map(
        per_device,
        mesh=split,
        in_specs=(slabs, slabs, slabs, slabs, P(), P(), P(), P(STATION), P(STATION)),
        out_specs=(slabs, P(), P(STATION), P(MP, STATION, None), P(None, MP, None, None)),
        check_vma=False,
    )
```

```python
import jax
import jax.numpy as jnp
from jax import lax
from jax.experimental import pallas as pl
from jax.experimental.pallas import tpu as pltpu
from jax.sharding import Mesh
from jax.sharding import PartitionSpec as P

MP = ("x", "z", "y_lo")
STATION = ("station_hi", "core")
MESH = MP + STATION
SPLIT = (4, 12, 2)
STENCIL = (-205.0 / 72.0, 8.0 / 5.0, -1.0 / 5.0, 8.0 / 315.0, -1.0 / 560.0)
TIME_RATIO = 0.1
MESH_ID = pl.DeviceIdType.MESH
SIDES = ((-1, 0), (1, 0), (0, -1), (0, 1), (-1, -1), (-1, 1), (1, -1), (1, 1))
ROW0 = 16
PLANE0 = 8


def place():
    x, z, low, high, core = (lax.axis_index(axis) for axis in MESH)
    nz = lax.axis_size("z")
    slab = (x * nz + z) * 2 + core
    return slab, high * 2 + low, low, core


def device_at(slab, block):
    nz = lax.axis_size("z")
    column = slab // 2
    return (column // nz, lax.rem(column, nz), lax.rem(block, 2), block // 2, lax.rem(slab, 2))


def advance(ref, prev, courant, mask, pulse, zmask, p0, planes, r0):
    rows = pl.ds(r0, 8)
    here = ref[pl.ds(p0, planes), rows, :]
    lap = 3.0 * STENCIL[0] * here
    for d in range(1, 5):
        pairs = ref[pl.ds(p0 + d, planes), rows, :] + ref[pl.ds(p0 - d, planes), rows, :]
        pairs = pairs + ref[pl.ds(p0, planes), pl.ds(r0 + d, 8), :]
        pairs = pairs + ref[pl.ds(p0, planes), pl.ds(r0 - d, 8), :]
        lap = lap + STENCIL[d] * pairs
        lap = lap + pltpu.roll(here, d, 2) * zmask[2 * d - 2][None]
        lap = lap + pltpu.roll(here, here.shape[2] - d, 2) * zmask[2 * d - 1][None]
    at = (pl.ds(p0, planes), rows)
    return 2.0 * here - prev[at] + courant[at] * lap + pulse * mask[at]


def total_of(parts):
    total = parts[0]
    for k in range(1, parts.shape[0]):
        total = total + parts[k]
    return total


def step_kernel(
    p_now, p_prev, velocity, density, wavelet, source, receivers, cells, observed,
    field, traces, residual, gradient, crossed,
    w, v, courant, mask, zmask, hits,
    init_send, init_recv, halo_send, halo_recv, tail_send, tail_recv,
    groups, stations, depth, tiles, sums, low_row, group_send, group_recv,
    models, model_send, model_recv,
    record_rows, early_z, early_x, early_y, late_z, late_x, late_y, ring_send, ring_recv,
):
    slab, block, low, core = place()
    slabs = lax.axis_size(MP)
    blocks = lax.axis_size("station_hi") * 2
    lateral, vertical = p_now.shape[1:]
    same = core == low
    inner = 1 - 2 * core
    outer = -inner
    pair = 1 - 2 * low

    def there(ds, db):
        return (slab + ds >= 0) & (slab + ds < slabs) & (block + db >= 0) & (block + db < blocks)

    def window(b):
        start = jnp.clip(8 * (b - 1), 0, lateral - 24)
        return pl.multiple_of(start, 8), pl.multiple_of(ROW0 + start - 8 * b, 8)

    zero = jnp.zeros((24, 24, vertical), jnp.float32)
    for ref in (w.at[0], w.at[1], v, courant):
        ref[:, pl.ds(8, 24), :] = zero

    for n in range(2):
        models[n, 0] = jnp.zeros(models.shape[2:], jnp.float32)
        models[n, 9] = jnp.zeros(models.shape[2:], jnp.float32)
        models[n, :, pl.ds(0, 8), :] = jnp.zeros((10, 8, vertical), jnp.float32)
        models[n, :, pl.ds(8 + lateral, 8), :] = jnp.zeros((10, 8, vertical), jnp.float32)

    barrier = pltpu.get_barrier_semaphore()
    for other in range(2 * blocks):
        b, k = other // 2, other % 2

        @pl.when((b != block) | (k != core))
        def _():
            pl.semaphore_signal(
                barrier, 1, device_id=device_at(slab - core + k, b), device_id_type=MESH_ID
            )

    for db in (-1, 0, 1):

        @pl.when(there(outer, db))
        def _():
            pl.semaphore_signal(
                barrier, 1, device_id=device_at(slab + outer, block + db), device_id_type=MESH_ID
            )

    x, z, high = lax.axis_index("x"), lax.axis_index("z"), block // 2
    nx, nz = lax.axis_size("x"), lax.axis_size("z")

    def on_z(k):
        return (x, k, low, high, core)

    def on_x(k):
        return (k // 2, z, low, high, lax.rem(k, 2))

    def on_y(k):
        return device_at(slab, k)

    me_z, me_x, me_y = z, 2 * x + core, block
    for d in range(1, nz):
        pl.semaphore_signal(
            barrier, 1, device_id=on_z(lax.rem(z + d, nz)), device_id_type=MESH_ID
        )
    for d in range(1, nx):
        for k in range(2):
            pl.semaphore_signal(
                barrier, 1, device_id=on_x(2 * lax.rem(x + d, nx) + k), device_id_type=MESH_ID
            )
    kept = (x * nz + z) * 2 + low
    onward = 2 * low - 1
    beyond = kept + onward
    more = (beyond >= 0) & (beyond < slabs)
    far = (beyond // (2 * nz), lax.rem(beyond // 2, nz), 1 - low, high, core)

    @pl.when(more)
    def _():
        pl.semaphore_signal(barrier, 1, device_id=far, device_id_type=MESH_ID)

    crossing = sum(jnp.where(there(outer, db), 1, 0) for db in (-1, 0, 1))
    pl.semaphore_wait(
        barrier, 2 * blocks - 1 + crossing + nz - 1 + 2 * (nx - 1) + jnp.where(more, 1, 0)
    )

    own_group = 2 * high + core
    sizes = (lateral.bit_length() - 1, lateral - 1)
    groups[own_group, pl.ds(0, 1), :] = (cells[...] >> sizes[0]).astype(jnp.float32)
    groups[own_group, pl.ds(1, 1), :] = (cells[...] & sizes[1]).astype(jnp.float32)
    groups[own_group, pl.ds(2, 1), :] = observed[...]

    def group_copy(d, forth):
        other = lax.rem(own_group + (d if forth else blocks - d), blocks)
        return pltpu.make_async_remote_copy(
            groups.at[own_group], groups.at[own_group if forth else other],
            group_send.at[d], group_recv.at[own_group if forth else other],
            device_id=(x, z, low, other // 2, lax.rem(other, 2)), device_id_type=MESH_ID,
        )

    for d in range(1, blocks):
        group_copy(d, True).start()

    arrays = (p_now, p_prev, velocity)
    places = (w.at[0], v, courant)

    def own_package(b, target, k):
        start, to = window(b)
        return [
            pltpu.make_async_remote_copy(
                a.at[:, pl.ds(start, 24), :],
                p.at[pl.ds(PLANE0, 8), pl.ds(to, 24), :],
                init_send.at[k, n], init_recv.at[0, n], device_id=target, device_id_type=MESH_ID,
            )
            for n, (a, p) in enumerate(zip(arrays, places))
        ]

    def halo_package(b, side, target, k, landing):
        start, to = window(b)
        left = side < 0
        near_from = jnp.where(left, 4, 0)
        near_to = jnp.where(left, 4, 16)
        rows = pl.multiple_of(8 * b, 8)
        copies = [
            pltpu.make_async_remote_copy(
                p_now.at[:, pl.ds(start, 24), :],
                w.at[0, pl.ds(jnp.where(left, 0, 16), 8), pl.ds(to, 24), :],
                init_send.at[k, 0], init_recv.at[landing, 0],
                device_id=target, device_id_type=MESH_ID,
            )
        ]
        for n in (1, 2):
            copies.append(
                pltpu.make_async_remote_copy(
                    arrays[n].at[pl.ds(near_from, 4), pl.ds(rows, 8), :],
                    places[n].at[pl.ds(near_to, 4), pl.ds(ROW0, 8), :],
                    init_send.at[k, n], init_recv.at[landing, n],
                    device_id=target, device_id_type=MESH_ID,
                )
            )
        return copies

    paired = block + pair
    partner = device_at(slab, paired)

    @pl.when(same)
    def _():
        for copy in own_package(paired, partner, 0):
            copy.start()
        for k, b in ((1, block), (2, paired)):

            @pl.when(there(outer, 0))
            def _():
                for copy in halo_package(b, -outer, device_at(slab + outer, b), k, 2):
                    copy.start()

    @pl.when(jnp.logical_not(same))
    def _():
        for copy in halo_package(paired, inner, partner, 0, 1):
            copy.start()

    start, to = window(block)
    rows = pl.multiple_of(8 * block, 8)

    def model_copy(n, outward, forth):
        e = onward if outward else -onward
        if forth:
            plane, landing = jnp.where(e > 0, 7, 0), jnp.where(e > 0, 0, 9)
        else:
            plane, landing = 0, jnp.where(e > 0, 9, 0)
        k = 1 if outward else 0
        return pltpu.make_async_remote_copy(
            (velocity, density)[n].at[plane], models.at[n, landing, pl.ds(8, lateral), :],
            model_send.at[n, k], model_recv.at[n, k],
            device_id=far if outward else partner, device_id_type=MESH_ID,
        )

    for n in range(2):
        model_copy(n, False, True).start()

        @pl.when(more)
        def _():
            model_copy(n, True, True).start()

        models[n, pl.ds(1, 8), pl.ds(8, lateral), :] = (velocity, density)[n][...]

    @pl.when(same)
    def _():
        for a, p in zip(arrays, places):
            p[pl.ds(PLANE0, 8), pl.ds(to, 24), :] = a[:, pl.ds(start, 24), :]

    @pl.when(jnp.logical_not(same))
    def _():
        left = inner < 0
        w[0, pl.ds(jnp.where(left, 0, 16), 8), pl.ds(to, 24), :] = p_now[:, pl.ds(start, 24), :]
        for a, p in ((p_prev, v), (velocity, courant)):
            p[pl.ds(jnp.where(left, 4, 16), 4), pl.ds(ROW0, 8), :] = a[
                pl.ds(jnp.where(left, 4, 0), 4), pl.ds(rows, 8), :
            ]

    source_cell = source[0]
    source_z = lax.rem(source_cell, vertical)
    source_xy = source_cell // vertical
    source_y = lax.rem(source_xy, lateral)
    source_x = source_xy // lateral
    shape = (24, 24, vertical)
    at_x = lax.broadcasted_iota(jnp.int32, shape, 0) + (8 * slab - PLANE0)
    at_y = lax.broadcasted_iota(jnp.int32, shape, 1) + (8 * block + 8 - ROW0)
    at_z = lax.broadcasted_iota(jnp.int32, shape, 2)
    hit = (at_x == source_x) & (at_y == source_y) & (at_z == source_z)
    mask[:, pl.ds(8, 24), :] = jnp.where(hit, 1.0, 0.0)
    lane = lax.broadcasted_iota(jnp.int32, (8, vertical), 1)
    for d in range(1, 5):
        zmask[2 * d - 2] = jnp.where(lane >= d, STENCIL[d], 0.0)
        zmask[2 * d - 1] = jnp.where(lane < vertical - d, STENCIL[d], 0.0)
    nrec = receivers.shape[1]
    cell = (8 * slab + lax.broadcasted_iota(jnp.int32, (8, 8, nrec), 0)) * lateral + (
        8 * block + lax.broadcasted_iota(jnp.int32, (8, 8, nrec), 1)
    )
    hits[...] = jnp.where(cell == receivers[...][None], 1.0, 0.0)

    step_z = lax.broadcasted_iota(jnp.int32, (vertical, 128), 0).astype(jnp.float32) + 1.0
    depth[0] = step_z
    depth[1] = step_z * step_z
    share = pl.multiple_of(8 * own_group, 8)
    sums[...] = jnp.zeros(sums.shape, jnp.float32)
    ngroups = groups.shape[0]

    def forward(q, unused):
        p, r = q // 4, 2 * lax.rem(q, 4)
        dx = (8 * kept + p).astype(jnp.float32) - stations[0]
        dz, dz_sq = depth[0], depth[1]
        for u in range(2):
            dy = (share + r + u).astype(jnp.float32) - stations[1]
            flat = dx * dx + dy * dy
            for g in range(ngroups):
                inverse = lax.rsqrt(flat[g : g + 1, :] + dz_sq)
                tile = (dz * inverse) * (inverse * inverse)
                tiles[q, pl.ds(u * vertical, vertical), pl.ds(g * 128, 128)] = tile.astype(
                    jnp.bfloat16
                )
        pair = jnp.concatenate(
            [density[p, pl.ds(share + r, 1), :], density[p, pl.ds(share + r + 1, 1), :]], axis=1
        )
        sums[...] += jnp.dot(
            pair.astype(jnp.bfloat16), tiles[q], preferred_element_type=jnp.float32
        )
        return unused

    def adjoint(q, unused):
        p, r = q // 4, 2 * lax.rem(q, 4)
        part = lax.dot_general(
            low_row[...].astype(jnp.bfloat16), tiles[q], (((1,), (1,)), ((), ())),
            preferred_element_type=jnp.float32,
        )
        gradient[p, pl.ds(r, 1), :] = part[:, :vertical]
        gradient[p, pl.ds(r + 1, 1), :] = part[:, vertical:]
        return unused

    def cross_plane(p, unused):
        lanes = lax.broadcasted_iota(jnp.int32, (lateral, vertical), 1)

        def slopes(f):
            mid = f[p + 1, pl.ds(8, lateral), :]
            along_x = (f[p + 2, pl.ds(8, lateral), :] - f[p, pl.ds(8, lateral), :]) * 0.5
            along_y = (f[p + 1, pl.ds(9, lateral), :] - f[p + 1, pl.ds(7, lateral), :]) * 0.5
            after = jnp.where(lanes < vertical - 1, pltpu.roll(mid, vertical - 1, 1), 0.0)
            before = jnp.where(lanes > 0, pltpu.roll(mid, 1, 1), 0.0)
            return along_x, along_y, (after - before) * 0.5

        vx, vy, vz = slopes(models.at[0])
        qx, qy, qz = slopes(models.at[1])
        crossed[0, p] = vy * qz - vz * qy
        crossed[1, p] = vz * qx - vx * qz
        crossed[2, p] = vx * qy - vy * qx
        return unused

    for d in range(1, blocks):
        group_copy(d, True).wait_send()
        group_copy(d, False).wait_recv()
    for g in range(ngroups):
        for n in range(3):
            stations[n, pl.ds(g, 1), :] = groups[g, pl.ds(n, 1), :]
    pairs_all = tiles.shape[0]
    quarter = pairs_all // 4
    lax.fori_loop(0, quarter, forward, 0)

    @pl.when(same)
    def _():
        for copy in own_package(paired, partner, 0):
            copy.wait_send()
        for k, b in ((1, block), (2, paired)):

            @pl.when(there(outer, 0))
            def _():
                for copy in halo_package(b, -outer, device_at(slab + outer, b), k, 2):
                    copy.wait_send()

        for copy in halo_package(block, inner, partner, 0, 1):
            copy.wait_recv()

    @pl.when(jnp.logical_not(same))
    def _():
        for copy in halo_package(paired, inner, partner, 0, 1):
            copy.wait_send()
        for copy in own_package(block, partner, 0):
            copy.wait_recv()

    @pl.when(there(outer, 0))
    def _():
        for copy in halo_package(block, outer, partner, 0, 2):
            copy.wait_recv()

    scaled = TIME_RATIO * courant[:, pl.ds(8, 24), :]
    courant[:, pl.ds(8, 24), :] = scaled * scaled

    def region(ds, db, near):
        plane = PLANE0 + 8 * ds
        count = 8
        if near and ds:
            plane, count = (4, 4) if ds < 0 else (16, 4)
        return pl.ds(plane, count), pl.ds(ROW0 + 8 * db, 8)

    def halo(slot, k):
        ds, db = SIDES[k]
        corner = ds != 0 and db != 0
        to = region(-ds, -db, corner)
        if corner:
            begin = (PLANE0, ROW0)[0] + (4 if ds > 0 else 0)
            source_at = (pl.ds(begin, 4), pl.ds(ROW0, 8))
        else:
            source_at = (pl.ds(PLANE0, 8), pl.ds(ROW0, 8))
        opposite = SIDES.index((-ds, -db))
        return pltpu.make_async_remote_copy(
            w.at[(slot, *source_at)], w.at[(slot, *to)],
            halo_send.at[k], halo_recv.at[slot, opposite],
            device_id=device_at(slab + ds, block + db), device_id_type=MESH_ID,
        )

    def arriving(slot, k):
        ds, db = SIDES[k]
        corner = ds != 0 and db != 0
        at = region(ds, db, corner)
        return pltpu.make_async_remote_copy(
            w.at[(slot, *at)], w.at[(slot, *at)],
            halo_send.at[k], halo_recv.at[slot, k],
            device_id=device_at(slab + ds, block + db), device_id_type=MESH_ID,
        )

    own = (pl.ds(PLANE0, 8), pl.ds(ROW0, 8))

    def record(values, n):
        top = jnp.broadcast_to(values[:, :, 0:1], values.shape)
        for half in range(nrec // 128):
            part = jnp.sum(top * hits[:, :, half * 128 : (half + 1) * 128], axis=0)
            row = n * (nrec // 128) + half
            record_rows[row // 8, pl.ds(lax.rem(row, 8), 1), :] = jnp.sum(part, axis=0, keepdims=True)

    def first(slot, m):
        pulse = wavelet[2 * m]
        here = w.at[slot]
        for p0 in (4, 16):
            new = advance(here, v, courant, mask, pulse, zmask, p0, 4, ROW0)
            v[pl.ds(p0, 4), pl.ds(ROW0, 8), :] = new
        for p0 in range(8, 16, 2):
            for r0 in (12, 20):
                new = advance(here, v, courant, mask, pulse, zmask, p0, 2, r0)
                v[pl.ds(p0, 2), pl.ds(r0, 8), :] = new

    def second(slot, m, target):
        pulse = wavelet[2 * m + 1]
        for p0 in range(8, 16, 2):
            new = advance(v, w.at[slot], courant, mask, pulse, zmask, p0, 2, ROW0)
            target[pl.ds(p0, 2), pl.ds(ROW0, 8), :] = new

    pairs = wavelet.shape[0] // 2

    def ring(k, buffer, me, n, address, forth, d):
        other = lax.rem(me + (d if forth else n - d), n)
        return pltpu.make_async_remote_copy(
            buffer.at[me], buffer.at[me if forth else other],
            ring_send.at[k, d], ring_recv.at[k, me if forth else other],
            device_id=address(other), device_id_type=MESH_ID,
        )

    def spread(k, buffer, me, address):
        for d in range(1, buffer.shape[0]):
            ring(k, buffer, me, buffer.shape[0], address, True, d).start()

    def gathered(k, buffer, me, address):
        for d in range(1, buffer.shape[0]):
            ring(k, buffer, me, buffer.shape[0], address, True, d).wait_send()
            ring(k, buffer, me, buffer.shape[0], address, False, d).wait_recv()
        return total_of(buffer)

    def step(m, background):
        slot = lax.rem(m, 2)
        later = 1 - slot
        first(slot, m)
        second(slot, m, w.at[later])
        for k, (ds, db) in enumerate(SIDES):

            @pl.when(there(ds, db))
            def _():
                halo(later, k).start()

        record(v[own], 2 * m)
        record(w[(later, *own)], 2 * m + 1)
        background()
        for k, (ds, db) in enumerate(SIDES):

            @pl.when(there(ds, db))
            def _():
                halo(later, k).wait_send()
                arriving(later, k).wait_recv()

    def body(m, unused):
        step(m, lambda: lax.fori_loop(quarter * (m + 1), quarter * (m + 2), forward, 0))
        return unused

    lax.fori_loop(0, 3, body, 0)

    def background_3():
        for g in range(ngroups):
            early_z[me_z, 0, pl.ds(g, 1), :] = sums[:, pl.ds(g * 128, 128)]
        early_z[me_z, 1] = record_rows[0]
        early_z[me_z, 2] = record_rows[1]
        spread(0, early_z, me_z, on_z)
        for n in range(2):
            for outward in (False, True):

                @pl.when(more | (not outward))
                def _():
                    model_copy(n, outward, True).wait_send()
                    model_copy(n, outward, False).wait_recv()

        lax.fori_loop(0, 8, cross_plane, 0)

    def background_4():
        early_x[me_x] = gathered(0, early_z, me_z, on_z)
        spread(1, early_x, me_x, on_x)

    def background_5():
        early_y[me_y] = gathered(1, early_x, me_x, on_x)
        spread(2, early_y, me_y, on_y)

    def put_traces(rows_at, first_step):
        for n in range(4):
            for half in range(2):
                traces[pl.ds(first_step + n, 1), pl.ds(128 * half, 128)] = rows_at[
                    2 * n + half : 2 * n + half + 1, :
                ]

    def background_6():
        total = gathered(2, early_y, me_y, on_y)
        left_over = total[0, :ngroups] - stations[2]
        stations[0] = left_over
        residual[...] = stations[0, pl.ds(own_group, 1), :]
        for g in range(ngroups):
            low_row[:, pl.ds(g * 128, 128)] = left_over[g : g + 1, :]
        put_traces(total[1], 0)
        put_traces(total[2], 4)
        lax.fori_loop(0, pairs_all, adjoint, 0)

    step(3, background_3)
    step(4, background_4)
    step(5, background_5)
    step(6, background_6)
    slot = (pairs - 1) % 2
    first(slot, pairs - 1)
    second(slot, pairs - 1, w.at[1 - slot])
    last = w.at[1 - slot]

    def handing(to, k):
        return pltpu.make_async_remote_copy(
            last.at[own], field.at[:, pl.ds(rows, 8), :],
            tail_send.at[to, k], tail_recv.at[block],
            device_id=(*device_at(slab, 2 * to + core)[:4], k), device_id_type=MESH_ID,
        )

    for to in range(blocks // 2):
        for k in range(2):

            @pl.when((2 * to + core != block) | (k != core))
            def _():
                handing(to, k).start()

    @pl.when(same)
    def _():
        field[:, pl.ds(rows, 8), :] = last[own]

    record(v[own], 2 * pairs - 2)
    record(last[own], 2 * pairs - 1)
    late_z[me_z, 0] = record_rows[2]
    late_z[me_z, 1] = record_rows[3]
    spread(3, late_z, me_z, on_z)
    late_x[me_x] = gathered(3, late_z, me_z, on_z)
    spread(4, late_x, me_x, on_x)
    late_y[me_y] = gathered(4, late_x, me_x, on_x)
    spread(5, late_y, me_y, on_y)
    total = gathered(5, late_y, me_y, on_y)
    put_traces(total[0], 8)
    put_traces(total[1], 12)
    for to in range(blocks // 2):
        for k in range(2):

            @pl.when((2 * to + core != block) | (k != core))
            def _():
                handing(to, k).wait_send()

    for b in range(blocks):

        @pl.when((b != block) | jnp.logical_not(same))
        def _():
            pltpu.make_async_remote_copy(
                last.at[own], field.at[:, pl.ds(8 * b, 8), :],
                tail_send.at[0, 0], tail_recv.at[b],
                device_id=partner, device_id_type=MESH_ID,
            ).wait_recv()


def per_device(
    p_now, p_prev, velocity, density, wavelet, source_cell, receiver_cells, station_cells, observed
):
    planes, lateral, vertical = p_now.shape
    nrec = receiver_cells.shape[0]
    blocks = lax.axis_size("station_hi") * 2
    nx, nz = lax.axis_size("x"), lax.axis_size("z")
    group = station_cells.shape[0]
    f32 = jnp.float32
    padded = (24, 40, vertical)
    vmem, smem = (pl.BlockSpec(memory_space=space) for space in (pltpu.VMEM, pltpu.SMEM))
    dma = pltpu.SemaphoreType.DMA
    longest = max(nz, 2 * nx, blocks)
    results = pl.pallas_call(
        step_kernel,
        out_shape=(
            jax.ShapeDtypeStruct(p_now.shape, f32),
            jax.ShapeDtypeStruct((wavelet.shape[0], nrec), f32),
            jax.ShapeDtypeStruct((1, group), f32),
            jax.ShapeDtypeStruct((planes, lateral // blocks, vertical), f32),
            jax.ShapeDtypeStruct((3, *p_now.shape), f32),
        ),
        in_specs=[vmem, vmem, vmem, vmem, smem, smem, vmem, vmem, vmem],
        out_specs=(vmem,) * 5,
        scratch_shapes=[
            pltpu.VMEM((2, *padded), f32),
            pltpu.VMEM(padded, f32),
            pltpu.VMEM(padded, f32),
            pltpu.VMEM(padded, f32),
            pltpu.VMEM((8, 8, vertical), f32),
            pltpu.VMEM((8, 8, nrec), f32),
            dma((3, 3)), dma((3, 3)), dma((8,)), dma((2, 8)), dma((blocks // 2, 2)), dma((blocks,)),
            pltpu.VMEM((blocks, 8, group), f32),
            pltpu.VMEM((3, blocks, group), f32),
            pltpu.VMEM((2, vertical, 128), f32),
            pltpu.VMEM((planes * 4, 2 * vertical, blocks * group), jnp.bfloat16),
            pltpu.VMEM((1, blocks * group), f32),
            pltpu.VMEM((1, blocks * group), f32),
            dma((blocks,)), dma((blocks,)),
            pltpu.VMEM((2, planes + 2, lateral + 16, vertical), f32),
            dma((2, 2)), dma((2, 2)),
            pltpu.VMEM((4, 8, 128), f32),
            *(pltpu.VMEM((n, 3, 8, 128), f32) for n in (nz, 2 * nx, blocks)),
            *(pltpu.VMEM((n, 2, 8, 128), f32) for n in (nz, 2 * nx, blocks)),
            dma((6, longest)), dma((6, longest)),
        ],
        compiler_params=pltpu.CompilerParams(
            collective_id=0, has_side_effects=True, vmem_limit_bytes=48 * 2**20
        ),
    )(
        p_now, p_prev, velocity, density, wavelet, source_cell,
        receiver_cells.reshape(1, -1), station_cells.reshape(1, -1), observed.reshape(1, -1),
    )
    field, traces, residual, gradient, crossed = results
    return field, traces, residual.reshape(-1), gradient, crossed


def solution(mesh):
    split = Mesh(mesh.devices.reshape(*SPLIT, mesh.shape["station"] // 2, 2), MESH)
    slabs = P(MP, None, None)
    return jax.shard_map(
        per_device,
        mesh=split,
        in_specs=(slabs, slabs, slabs, slabs, P(), P(), P(), P(STATION), P(STATION)),
        out_specs=(slabs, P(), P(STATION), P(MP, STATION, None), P(None, MP, None, None)),
        check_vma=False,
    )
```

```python
import jax
import jax.numpy as jnp
from jax import lax
from jax.experimental import pallas as pl
from jax.experimental.pallas import tpu as pltpu
from jax.sharding import Mesh
from jax.sharding import PartitionSpec as P

MP = ("x", "z", "y_lo")
STATION = ("station_hi", "core")
MESH = MP + STATION
SPLIT = (4, 12, 2)
STENCIL = (-205.0 / 72.0, 8.0 / 5.0, -1.0 / 5.0, 8.0 / 315.0, -1.0 / 560.0)
TIME_RATIO = 0.1
MESH_ID = pl.DeviceIdType.MESH
SIDES = ((-1, 0), (1, 0), (0, -1), (0, 1), (-1, -1), (-1, 1), (1, -1), (1, 1))
ROW0 = 16
PLANE0 = 8


def place():
    x, z, low, high, core = (lax.axis_index(axis) for axis in MESH)
    nz = lax.axis_size("z")
    slab = (x * nz + z) * 2 + core
    return slab, high * 2 + low, low, core


def device_at(slab, block):
    nz = lax.axis_size("z")
    column = slab // 2
    return (column // nz, lax.rem(column, nz), lax.rem(block, 2), block // 2, lax.rem(slab, 2))


def advance(ref, prev, courant, mask, pulse, zmask, p0, planes, r0):
    rows = pl.ds(r0, 8)
    here = ref[pl.ds(p0, planes), rows, :]
    lap = 3.0 * STENCIL[0] * here
    for d in range(1, 5):
        pairs = ref[pl.ds(p0 + d, planes), rows, :] + ref[pl.ds(p0 - d, planes), rows, :]
        pairs = pairs + ref[pl.ds(p0, planes), pl.ds(r0 + d, 8), :]
        pairs = pairs + ref[pl.ds(p0, planes), pl.ds(r0 - d, 8), :]
        lap = lap + STENCIL[d] * pairs
        lap = lap + pltpu.roll(here, d, 2) * zmask[2 * d - 2][None]
        lap = lap + pltpu.roll(here, here.shape[2] - d, 2) * zmask[2 * d - 1][None]
    at = (pl.ds(p0, planes), rows)
    return 2.0 * here - prev[at] + courant[at] * lap + pulse * mask[at]


def total_of(parts):
    total = parts[0]
    for k in range(1, parts.shape[0]):
        total = total + parts[k]
    return total


def step_kernel(
    p_now, p_prev, velocity, density, wavelet, source, receivers, cells, observed,
    field, traces, residual, gradient, crossed,
    w, v, courant, mask, zmask, hits,
    init_send, init_recv, halo_send, halo_recv, tail_send, tail_recv,
    groups, stations, depth, tiles, sums, low_row, group_send, group_recv,
    models, model_send, model_recv, local,
    record_rows, early_z, early_x, early_y, late_z, late_x, late_y, end_z, end_x, end_y,
    ring_send, ring_recv, corner_out, corner_in, spreading,
):
    slab, block, low, core = place()
    slabs = lax.axis_size(MP)
    blocks = lax.axis_size("station_hi") * 2
    lateral, vertical = p_now.shape[1:]
    same = core == low
    inner = 1 - 2 * core
    outer = -inner
    pair = 1 - 2 * low

    def there(ds, db):
        return (slab + ds >= 0) & (slab + ds < slabs) & (block + db >= 0) & (block + db < blocks)

    def window(b):
        start = jnp.clip(8 * (b - 1), 0, lateral - 24)
        return pl.multiple_of(start, 8), pl.multiple_of(ROW0 + start - 8 * b, 8)

    barrier = pltpu.get_barrier_semaphore()
    for other in range(2 * blocks):
        b, k = other // 2, other % 2

        @pl.when((b != block) | (k != core))
        def _():
            pl.semaphore_signal(
                barrier, 1, device_id=device_at(slab - core + k, b), device_id_type=MESH_ID
            )

    for db in (-1, 0, 1):

        @pl.when(there(outer, db))
        def _():
            pl.semaphore_signal(
                barrier, 1, device_id=device_at(slab + outer, block + db), device_id_type=MESH_ID
            )

    x, z, high = lax.axis_index("x"), lax.axis_index("z"), block // 2
    nx, nz = lax.axis_size("x"), lax.axis_size("z")

    def on_z(k):
        return (x, k, low, high, core)

    def on_x(k):
        return (k // 2, z, low, high, lax.rem(k, 2))

    def on_y(k):
        return device_at(slab, k)

    me_z, me_x, me_y = z, 2 * x + core, block
    for d in range(1, nz):
        pl.semaphore_signal(
            barrier, 1, device_id=on_z(lax.rem(z + d, nz)), device_id_type=MESH_ID
        )
    for d in range(1, nx):
        for k in range(2):
            pl.semaphore_signal(
                barrier, 1, device_id=on_x(2 * lax.rem(x + d, nx) + k), device_id_type=MESH_ID
            )
    kept = (x * nz + z) * 2 + low
    onward = 2 * low - 1
    beyond = kept + onward
    more = (beyond >= 0) & (beyond < slabs)
    far = (beyond // (2 * nz), lax.rem(beyond // 2, nz), 1 - low, high, core)

    @pl.when(more)
    def _():
        pl.semaphore_signal(barrier, 1, device_id=far, device_id_type=MESH_ID)

    start, to = window(block)
    rows = pl.multiple_of(8 * block, 8)
    inside = (pl.ds(1, 8), pl.ds(8, lateral))
    loads = [
        pltpu.make_async_copy(density, models.at[(1, *inside)], local.at[3]),
        pltpu.make_async_copy(velocity, models.at[(0, *inside)], local.at[4]),
    ]
    for copy in loads:
        copy.start()
    inner_left = inner < 0

    def local_copies(own_slab):
        if own_slab:
            pairs_of = [
                (a.at[:, pl.ds(start, 24), :], p.at[pl.ds(PLANE0, 8), pl.ds(to, 24), :])
                for a, p in ((p_now, w.at[0]), (p_prev, v), (velocity, courant))
            ]
        else:
            pairs_of = [
                (
                    p_now.at[:, pl.ds(start, 24), :],
                    w.at[0, pl.ds(jnp.where(inner_left, 0, 16), 8), pl.ds(to, 24), :],
                )
            ] + [
                (
                    a.at[pl.ds(jnp.where(inner_left, 4, 0), 4), pl.ds(rows, 8), :],
                    p.at[pl.ds(jnp.where(inner_left, 4, 16), 4), pl.ds(ROW0, 8), :],
                )
                for a, p in ((p_prev, v), (velocity, courant))
            ]
        return [
            pltpu.make_async_copy(a, b, local.at[n]) for n, (a, b) in enumerate(pairs_of)
        ]

    @pl.when(same)
    def _():
        for copy in local_copies(True):
            copy.start()

    @pl.when(jnp.logical_not(same))
    def _():
        for copy in local_copies(False):
            copy.start()

    def clear(at):
        shape = (at[0].size, at[1].size, vertical)
        for ref in (w.at[0], w.at[1], v, courant):
            ref[at] = jnp.zeros(shape, jnp.float32)

    pl.when(slab == 0)(lambda: clear((pl.ds(0, 8), pl.ds(8, 24))))
    pl.when(slab == slabs - 1)(lambda: clear((pl.ds(16, 8), pl.ds(8, 24))))
    pl.when(block == 0)(lambda: clear((pl.ds(0, 24), pl.ds(8, 8))))
    pl.when(block == blocks - 1)(lambda: clear((pl.ds(0, 24), pl.ds(24, 8))))
    for n in range(2):
        for plane in (0, 9):

            @pl.when(kept == (0 if plane == 0 else slabs - 1))
            def _():
                models[n, plane, pl.ds(8, lateral), :] = jnp.zeros((lateral, vertical), jnp.float32)

        for row in (0, 8 + lateral):
            models[n, :, pl.ds(row, 8), :] = jnp.zeros((10, 8, vertical), jnp.float32)

    crossing = sum(jnp.where(there(outer, db), 1, 0) for db in (-1, 0, 1))
    pl.semaphore_wait(
        barrier, 2 * blocks - 1 + crossing + nz - 1 + 2 * (nx - 1) + jnp.where(more, 1, 0)
    )

    own_group = 2 * high + core
    sizes = (lateral.bit_length() - 1, lateral - 1)
    groups[own_group, pl.ds(0, 1), :] = (cells[...] >> sizes[0]).astype(jnp.float32)
    groups[own_group, pl.ds(1, 1), :] = (cells[...] & sizes[1]).astype(jnp.float32)
    groups[own_group, pl.ds(2, 1), :] = observed[...]

    def group_copy(d, forth):
        other = lax.rem(own_group + (d if forth else blocks - d), blocks)
        return pltpu.make_async_remote_copy(
            groups.at[own_group], groups.at[own_group if forth else other],
            group_send.at[d], group_recv.at[own_group if forth else other],
            device_id=(x, z, low, other // 2, lax.rem(other, 2)), device_id_type=MESH_ID,
        )

    for d in range(1, blocks):
        group_copy(d, True).start()

    arrays = (p_now, p_prev, velocity)
    places = (w.at[0], v, courant)

    def own_package(n, b, target):
        begin, landing = window(b)
        return pltpu.make_async_remote_copy(
            arrays[n].at[:, pl.ds(begin, 24), :],
            places[n].at[pl.ds(PLANE0, 8), pl.ds(landing, 24), :],
            init_send.at[3, n], init_recv.at[0, n], device_id=target, device_id_type=MESH_ID,
        )

    def halo_package(b, side, target, k, landing):
        begin, to_row = window(b)
        left = side < 0
        near, far_off = jnp.where(left, 4, 0), jnp.where(left, 0, 4)
        near_to, far_to = jnp.where(left, 4, 16), jnp.where(left, 0, 20)
        home = pl.multiple_of(8 * b, 8)
        block_at, block_to = pl.ds(home, 8), pl.ds(ROW0, 8)
        parts = [
            (p_now.at[pl.ds(near, 4), pl.ds(begin, 24), :], w.at[0, pl.ds(near_to, 4), pl.ds(to_row, 24), :]),
            (p_now.at[pl.ds(far_off, 4), block_at, :], w.at[0, pl.ds(far_to, 4), block_to, :]),
        ] + [
            (a.at[pl.ds(near, 4), block_at, :], p.at[pl.ds(near_to, 4), block_to, :])
            for a, p in ((p_prev, v), (velocity, courant))
        ]
        return [
            pltpu.make_async_remote_copy(
                a, p, init_send.at[k, n], init_recv.at[landing, n],
                device_id=target, device_id_type=MESH_ID,
            )
            for n, (a, p) in enumerate(parts)
        ]

    paired = block + pair
    across = lax.rem(block - pair + blocks, blocks)
    partner = device_at(slab, paired)

    @pl.when(same)
    def _():
        own_package(0, paired, partner).start()
        for n in (1, 2):
            own_package(n, across, device_at(slab, across)).start()
        for k, b in ((1, block), (2, paired)):

            @pl.when(there(outer, 0))
            def _():
                for copy in halo_package(b, -outer, device_at(slab + outer, b), k, 2):
                    copy.start()

    @pl.when(jnp.logical_not(same))
    def _():
        for copy in halo_package(paired, inner, partner, 0, 1):
            copy.start()

    def model_copy(n, outward, forth):
        e = onward if outward else -onward
        if forth:
            plane, landing = jnp.where(e > 0, 7, 0), jnp.where(e > 0, 0, 9)
        else:
            plane, landing = 0, jnp.where(e > 0, 9, 0)
        k = 1 if outward else 0
        return pltpu.make_async_remote_copy(
            (velocity, density)[n].at[plane], models.at[n, landing, pl.ds(8, lateral), :],
            model_send.at[n, k], model_recv.at[n, k],
            device_id=far if outward else partner, device_id_type=MESH_ID,
        )

    source_cell = source[0]
    source_z = lax.rem(source_cell, vertical)
    source_xy = source_cell // vertical
    source_y = lax.rem(source_xy, lateral)
    source_x = source_xy // lateral
    shape = (24, 24, vertical)
    at_x = lax.broadcasted_iota(jnp.int32, shape, 0) + (8 * slab - PLANE0)
    at_y = lax.broadcasted_iota(jnp.int32, shape, 1) + (8 * block + 8 - ROW0)
    at_z = lax.broadcasted_iota(jnp.int32, shape, 2)
    hit = (at_x == source_x) & (at_y == source_y) & (at_z == source_z)
    mask[:, pl.ds(8, 24), :] = jnp.where(hit, 1.0, 0.0)
    lane = lax.broadcasted_iota(jnp.int32, (8, vertical), 1)
    for d in range(1, 5):
        zmask[2 * d - 2] = jnp.where(lane >= d, STENCIL[d], 0.0)
        zmask[2 * d - 1] = jnp.where(lane < vertical - d, STENCIL[d], 0.0)
    nrec = receivers.shape[1]
    cell = (8 * slab + lax.broadcasted_iota(jnp.int32, (8, 8, nrec), 0)) * lateral + (
        8 * block + lax.broadcasted_iota(jnp.int32, (8, 8, nrec), 1)
    )
    hits[...] = jnp.where(cell == receivers[...][None], 1.0, 0.0)

    step_z = lax.broadcasted_iota(jnp.int32, (vertical, 128), 0).astype(jnp.float32) + 1.0
    depth[0] = step_z
    depth[1] = step_z * step_z
    share = pl.multiple_of(8 * own_group, 8)
    ngroups = groups.shape[0]
    sums[...] = jnp.zeros(sums.shape, jnp.float32)
    record_rows[3] = jnp.zeros((8, 128), jnp.float32)
    eye = lax.broadcasted_iota(jnp.int32, (128, 128), 0) == lax.broadcasted_iota(
        jnp.int32, (128, 128), 1
    )

    def column(row):
        picked = jnp.where(eye, jnp.broadcast_to(row, (128, 128)), 0.0).astype(jnp.bfloat16)
        ones = jnp.ones((128, 128), jnp.bfloat16)
        return jnp.dot(picked, ones, preferred_element_type=jnp.float32)

    def forward(q, unused):
        p, r = q // 4, 2 * lax.rem(q, 4)
        dx = (8 * kept + p).astype(jnp.float32) - stations[0]
        for u in range(2):
            dy = (share + r + u).astype(jnp.float32) - stations[1]
            flat = dx * dx + dy * dy
            weight = column(models[1, p + 1, pl.ds(8 + share + r + u, 1), :])
            for g in range(ngroups):
                inverse = lax.rsqrt(flat[g : g + 1, :] + depth[1])
                tile = ((depth[0] * inverse) * (inverse * inverse)).astype(jnp.bfloat16)
                tiles[q, pl.ds(u * vertical, vertical), pl.ds(g * 128, 128)] = tile
                part = tile.astype(jnp.float32) * weight
                sums[g] += jnp.sum(part.reshape(vertical // 8, 8, 128), axis=0)
        return unused

    def adjoint(p, unused):
        each = tiles.shape[0] // 8
        slab_tiles = tiles[pl.ds(p * each, each)].reshape(each * 2 * vertical, ngroups * 128)
        out = jnp.dot(slab_tiles, spreading[...], preferred_element_type=jnp.float32)
        for r in range(2 * each):
            unit = jnp.where(eye, out[vertical * r : vertical * (r + 1)], 0.0)
            part = jnp.sum(unit.reshape(vertical // 8, 8, 128), axis=0)
            gradient[p, pl.ds(r, 1), :] = jnp.sum(part, axis=0, keepdims=True)
        return unused

    def cross_plane(p, unused):
        lanes = lax.broadcasted_iota(jnp.int32, (lateral, vertical), 1)

        def slopes(f):
            mid = f[p + 1, pl.ds(8, lateral), :]
            along_x = (f[p + 2, pl.ds(8, lateral), :] - f[p, pl.ds(8, lateral), :]) * 0.5
            along_y = (f[p + 1, pl.ds(9, lateral), :] - f[p + 1, pl.ds(7, lateral), :]) * 0.5
            after = jnp.where(lanes < vertical - 1, pltpu.roll(mid, vertical - 1, 1), 0.0)
            before = jnp.where(lanes > 0, pltpu.roll(mid, 1, 1), 0.0)
            return along_x, along_y, (after - before) * 0.5

        vx, vy, vz = slopes(models.at[0])
        qx, qy, qz = slopes(models.at[1])
        crossed[0, p] = vy * qz - vz * qy
        crossed[1, p] = vz * qx - vx * qz
        crossed[2, p] = vx * qy - vy * qx
        return unused

    loads[0].wait()
    for d in range(1, blocks):
        group_copy(d, True).wait_send()
        group_copy(d, False).wait_recv()
    for g in range(ngroups):
        for n in range(3):
            stations[n, pl.ds(g, 1), :] = groups[g, pl.ds(n, 1), :]
    pairs_all = tiles.shape[0]
    quarter = pairs_all // 4
    lax.fori_loop(0, quarter, forward, 0)

    @pl.when(same)
    def _():
        own_package(0, paired, partner).wait_send()
        for n in (1, 2):
            own_package(n, across, device_at(slab, across)).wait_send()
        for k, b in ((1, block), (2, paired)):

            @pl.when(there(outer, 0))
            def _():
                for copy in halo_package(b, -outer, device_at(slab + outer, b), k, 2):
                    copy.wait_send()

        for copy in halo_package(block, inner, partner, 0, 1):
            copy.wait_recv()
        for copy in local_copies(True):
            copy.wait()

    @pl.when(jnp.logical_not(same))
    def _():
        for copy in halo_package(paired, inner, partner, 0, 1):
            copy.wait_send()
        for n in range(3):
            own_package(n, block, partner).wait_recv()
        for copy in local_copies(False):
            copy.wait()

    @pl.when(there(outer, 0))
    def _():
        for copy in halo_package(block, outer, partner, 0, 2):
            copy.wait_recv()

    scaled = TIME_RATIO * courant[:, pl.ds(8, 24), :]
    courant[:, pl.ds(8, 24), :] = scaled * scaled

    order = (4, 5, 6, 7, 2, 3, 0, 1)

    def halo(slot, k, forth):
        ds, db = SIDES[k]
        opposite = SIDES.index((-ds, -db))
        if k >= 4:
            begin = corner_out.at[k - 4]
            end = corner_in.at[slot, (opposite if forth else k) - 4]
        else:
            begin = w.at[slot, pl.ds(PLANE0, 8), pl.ds(ROW0, 8), :]
            sign = -1 if forth else 1
            end = w.at[
                slot, pl.ds(PLANE0 + 8 * sign * ds, 8), pl.ds(ROW0 + 8 * sign * db, 8), :
            ]
        return pltpu.make_async_remote_copy(
            begin, end, halo_send.at[k], halo_recv.at[slot, opposite if forth else k],
            device_id=device_at(slab + ds, block + db), device_id_type=MESH_ID,
        )

    def corner_rows(k, outside):
        ds, db = SIDES[k]
        plane = (16 if ds > 0 else 4) if outside else (12 if ds > 0 else 8)
        row = (24 if db > 0 else 12) if outside else (20 if db > 0 else 16)
        return plane, row

    def stage_corner(slot, k):
        plane, row = corner_rows(k, False)
        for n in range(4):
            corner_out[k - 4, n // 2, pl.ds(4 * (n % 2), 4), :] = w[slot, plane + n, pl.ds(row, 4), :]

    def place_corner(slot, k):
        plane, row = corner_rows(k, True)
        for n in range(4):
            w[slot, plane + n, pl.ds(row, 4), :] = corner_in[slot, k - 4, n // 2, pl.ds(4 * (n % 2), 4), :]

    own = (pl.ds(PLANE0, 8), pl.ds(ROW0, 8))

    def record(values, n):
        top = jnp.broadcast_to(values[:, :, 0:1], values.shape)
        for half in range(nrec // 128):
            part = jnp.sum(top * hits[:, :, half * 128 : (half + 1) * 128], axis=0)
            row = n * (nrec // 128) + half
            record_rows[row // 8, pl.ds(lax.rem(row, 8), 1), :] = jnp.sum(part, axis=0, keepdims=True)

    def first(slot, m):
        pulse = wavelet[2 * m]
        here = w.at[slot]
        for p0 in (4, 16):
            new = advance(here, v, courant, mask, pulse, zmask, p0, 4, ROW0)
            v[pl.ds(p0, 4), pl.ds(ROW0, 8), :] = new
        for p0 in range(8, 16, 2):
            for r0 in (12, 20):
                new = advance(here, v, courant, mask, pulse, zmask, p0, 2, r0)
                v[pl.ds(p0, 2), pl.ds(r0, 8), :] = new

    def second(slot, m, target):
        pulse = wavelet[2 * m + 1]
        for p0 in range(8, 16, 2):
            new = advance(v, w.at[slot], courant, mask, pulse, zmask, p0, 2, ROW0)
            target[pl.ds(p0, 2), pl.ds(ROW0, 8), :] = new

    pairs = wavelet.shape[0] // 2

    def ring(k, buffer, me, n, address, forth, d):
        other = lax.rem(me + (d if forth else n - d), n)
        return pltpu.make_async_remote_copy(
            buffer.at[me], buffer.at[me if forth else other],
            ring_send.at[k, d], ring_recv.at[k, me if forth else other],
            device_id=address(other), device_id_type=MESH_ID,
        )

    def spread(k, buffer, me, address):
        for d in range(1, buffer.shape[0]):
            ring(k, buffer, me, buffer.shape[0], address, True, d).start()

    def gathered(k, buffer, me, address):
        for d in range(1, buffer.shape[0]):
            ring(k, buffer, me, buffer.shape[0], address, True, d).wait_send()
            ring(k, buffer, me, buffer.shape[0], address, False, d).wait_recv()
        return total_of(buffer)

    def step(m, background):
        slot = lax.rem(m, 2)
        later = 1 - slot
        first(slot, m)
        second(slot, m, w.at[later])
        for k in range(4, 8):
            stage_corner(later, k)
        for k in order:

            @pl.when(there(*SIDES[k]))
            def _():
                halo(later, k, True).start()

        record(v[own], 2 * m)
        record(w[(later, *own)], 2 * m + 1)
        background()
        for k in (0, 1, 2, 3, 4, 5, 6, 7):

            @pl.when(there(*SIDES[k]))
            def _():
                halo(later, k, True).wait_send()
                halo(later, k, False).wait_recv()
                if k >= 4:
                    place_corner(later, k)

    def model_ways():
        for n in range(2):
            for outward in (False, True):
                yield n, outward, (more if outward else more | True)

    def body(m, unused):
        def background():
            @pl.when(m == 0)
            def _():
                for n, outward, really in model_ways():

                    @pl.when(really)
                    def _():
                        model_copy(n, outward, True).start()

            lax.fori_loop(quarter * (m + 1), quarter * (m + 2), forward, 0)

        step(m, background)
        return unused

    lax.fori_loop(0, 3, body, 0)

    def background_3():
        for g in range(ngroups):
            early_z[me_z, 0, pl.ds(g, 1), :] = jnp.sum(sums[g], axis=0, keepdims=True)
        early_z[me_z, 1] = record_rows[0]
        early_z[me_z, 2] = record_rows[1]
        spread(0, early_z, me_z, on_z)

    def background_4():
        loads[1].wait()
        for n, outward, really in model_ways():

            @pl.when(really)
            def _():
                model_copy(n, outward, True).wait_send()
                model_copy(n, outward, False).wait_recv()

        lax.fori_loop(0, 8, cross_plane, 0)

    def background_5():
        early_x[me_x] = gathered(0, early_z, me_z, on_z)
        spread(1, early_x, me_x, on_x)

    def background_6():
        late_z[me_z, 0] = record_rows[2]
        late_z[me_z, 1] = record_rows[3]
        spread(3, late_z, me_z, on_z)
        early_y[me_y] = gathered(1, early_x, me_x, on_x)
        spread(2, early_y, me_y, on_y)

    def put_traces(rows_at, first_step, count):
        for n in range(count):
            for half in range(2):
                traces[pl.ds(first_step + n, 1), pl.ds(128 * half, 128)] = rows_at[
                    2 * n + half : 2 * n + half + 1, :
                ]

    step(3, background_3)
    step(4, background_4)
    step(5, background_5)
    step(6, background_6)
    slot = (pairs - 1) % 2
    first(slot, pairs - 1)
    second(slot, pairs - 1, w.at[1 - slot])
    last = w.at[1 - slot]

    def handing(to, k):
        return pltpu.make_async_remote_copy(
            last.at[own], field.at[:, pl.ds(rows, 8), :],
            tail_send.at[to, k], tail_recv.at[block],
            device_id=(*device_at(slab, 2 * to + core)[:4], k), device_id_type=MESH_ID,
        )

    for to in range(blocks // 2):
        for k in range(2):

            @pl.when((2 * to + core != block) | (k != core))
            def _():
                handing(to, k).start()

    @pl.when(same)
    def _():
        field[:, pl.ds(rows, 8), :] = last[own]

    record(v[own], 2 * pairs - 2)
    record(last[own], 2 * pairs - 1)
    end_z[me_z] = record_rows[3, pl.ds(4, 4), :]
    spread(6, end_z, me_z, on_z)
    total = gathered(2, early_y, me_y, on_y)
    left_over = total[0, :ngroups] - stations[2]
    stations[0] = left_over
    residual[...] = stations[0, pl.ds(own_group, 1), :]
    for g in range(ngroups):
        spreading[pl.ds(128 * g, 128), :] = column(left_over[g : g + 1, :]).astype(jnp.bfloat16)
    put_traces(total[1], 0, 4)
    put_traces(total[2], 4, 4)
    late_x[me_x] = gathered(3, late_z, me_z, on_z)
    spread(4, late_x, me_x, on_x)
    lax.fori_loop(0, 5, adjoint, 0)
    end_x[me_x] = gathered(6, end_z, me_z, on_z)
    spread(7, end_x, me_x, on_x)
    late_y[me_y] = gathered(4, late_x, me_x, on_x)
    spread(5, late_y, me_y, on_y)
    lax.fori_loop(5, 8, adjoint, 0)
    end_y[me_y] = gathered(7, end_x, me_x, on_x)
    spread(8, end_y, me_y, on_y)
    total = gathered(5, late_y, me_y, on_y)
    put_traces(total[0], 8, 4)
    put_traces(total[1], 12, 2)
    put_traces(gathered(8, end_y, me_y, on_y), 14, 2)
    for to in range(blocks // 2):
        for k in range(2):

            @pl.when((2 * to + core != block) | (k != core))
            def _():
                handing(to, k).wait_send()

    for b in range(blocks):

        @pl.when((b != block) | jnp.logical_not(same))
        def _():
            pltpu.make_async_remote_copy(
                last.at[own], field.at[:, pl.ds(8 * b, 8), :],
                tail_send.at[0, 0], tail_recv.at[b],
                device_id=partner, device_id_type=MESH_ID,
            ).wait_recv()


def store_kernel(*refs):
    copies = [pltpu.make_async_copy(refs[n], refs[5 + n], refs[10].at[n]) for n in range(5)]
    for copy in copies:
        copy.start()
    for copy in copies:
        copy.wait()


def per_device(
    p_now, p_prev, velocity, density, wavelet, source_cell, receiver_cells, station_cells, observed
):
    planes, lateral, vertical = p_now.shape
    nrec = receiver_cells.shape[0]
    blocks = lax.axis_size("station_hi") * 2
    nx, nz = lax.axis_size("x"), lax.axis_size("z")
    group = station_cells.shape[0]
    f32 = jnp.float32
    padded = (24, 40, vertical)
    vmem, smem = (pl.BlockSpec(memory_space=space) for space in (pltpu.VMEM, pltpu.SMEM))
    hbm = pl.BlockSpec(memory_space=pltpu.HBM)
    dma = pltpu.SemaphoreType.DMA
    longest = max(nz, 2 * nx, blocks)
    results = pl.pallas_call(
        step_kernel,
        out_shape=(
            jax.ShapeDtypeStruct(p_now.shape, f32),
            jax.ShapeDtypeStruct((wavelet.shape[0], nrec), f32),
            jax.ShapeDtypeStruct((1, group), f32),
            jax.ShapeDtypeStruct((planes, lateral // blocks, vertical), f32),
            jax.ShapeDtypeStruct((3, *p_now.shape), f32),
        ),
        in_specs=[hbm, hbm, hbm, hbm, smem, smem, vmem, vmem, vmem],
        out_specs=(vmem,) * 5,
        scratch_shapes=[
            pltpu.VMEM((2, *padded), f32),
            pltpu.VMEM(padded, f32),
            pltpu.VMEM(padded, f32),
            pltpu.VMEM(padded, f32),
            pltpu.VMEM((8, 8, vertical), f32),
            pltpu.VMEM((8, 8, nrec), f32),
            dma((4, 4)), dma((3, 4)), dma((8,)), dma((2, 8)), dma((blocks // 2, 2)), dma((blocks,)),
            pltpu.VMEM((blocks, 8, group), f32),
            pltpu.VMEM((3, blocks, group), f32),
            pltpu.VMEM((2, vertical, 128), f32),
            pltpu.VMEM((planes * 4, 2 * vertical, blocks * group), jnp.bfloat16),
            pltpu.VMEM((blocks, 8, group), f32),
            pltpu.VMEM((1, blocks * group), f32),
            dma((blocks,)), dma((blocks,)),
            pltpu.VMEM((2, planes + 2, lateral + 16, vertical), f32),
            dma((2, 2)), dma((2, 2)), dma((5,)),
            pltpu.VMEM((4, 8, 128), f32),
            *(pltpu.VMEM((n, 3, 8, 128), f32) for n in (nz, 2 * nx, blocks)),
            *(pltpu.VMEM((n, 2, 8, 128), f32) for n in (nz, 2 * nx, blocks)),
            *(pltpu.VMEM((n, 4, 128), f32) for n in (nz, 2 * nx, blocks)),
            dma((9, longest)), dma((9, longest)),
            pltpu.VMEM((4, 2, 8, vertical), f32),
            pltpu.VMEM((2, 4, 2, 8, vertical), f32),
            pltpu.VMEM((blocks * group, 128), jnp.bfloat16),
        ],
        compiler_params=pltpu.CompilerParams(
            collective_id=0, has_side_effects=True, vmem_limit_bytes=48 * 2**20
        ),
    )(
        *(pltpu.with_memory_space_constraint(a, pltpu.HBM) for a in (p_now, p_prev, velocity, density)), wavelet, source_cell,
        receiver_cells.reshape(1, -1), station_cells.reshape(1, -1), observed.reshape(1, -1),
    )
    field, traces, residual, gradient, crossed = pl.pallas_call(
        store_kernel,
        out_shape=tuple(jax.ShapeDtypeStruct(r.shape, r.dtype) for r in results),
        in_specs=[vmem] * 5,
        out_specs=(hbm,) * 5,
        scratch_shapes=[dma((5,))],
        compiler_params=pltpu.CompilerParams(vmem_limit_bytes=2 * 2**20),
    )(*results)
    return field, traces, residual.reshape(-1), gradient, crossed


def solution(mesh):
    split = Mesh(mesh.devices.reshape(*SPLIT, mesh.shape["station"] // 2, 2), MESH)
    slabs = P(MP, None, None)
    return jax.shard_map(
        per_device,
        mesh=split,
        in_specs=(slabs, slabs, slabs, slabs, P(), P(), P(), P(STATION), P(STATION)),
        out_specs=(slabs, P(), P(STATION), P(MP, STATION, None), P(None, MP, None, None)),
        check_vma=False,
    )
```

```python
import jax
import jax.numpy as jnp
from jax import lax
from jax.experimental import pallas as pl
from jax.experimental.pallas import tpu as pltpu
from jax.sharding import Mesh
from jax.sharding import PartitionSpec as P

MP = ("x", "z", "y_lo")
STATION = ("station_hi", "core")
MESH = MP + STATION
SPLIT = (4, 12, 2)
STENCIL = (-205.0 / 72.0, 8.0 / 5.0, -1.0 / 5.0, 8.0 / 315.0, -1.0 / 560.0)
TIME_RATIO = 0.1
MESH_ID = pl.DeviceIdType.MESH
SIDES = ((-1, 0), (1, 0), (0, -1), (0, 1), (-1, -1), (-1, 1), (1, -1), (1, 1))
ROW0 = 16
PLANE0 = 8


def place():
    x, z, low, high, core = (lax.axis_index(axis) for axis in MESH)
    nz = lax.axis_size("z")
    slab = (x * nz + z) * 2 + core
    return slab, high * 2 + low, low, core


def device_at(slab, block):
    nz = lax.axis_size("z")
    column = slab // 2
    return (column // nz, lax.rem(column, nz), lax.rem(block, 2), block // 2, lax.rem(slab, 2))


def advance(ref, prev, courant, mask, pulse, zmask, p0, planes, r0):
    rows = pl.ds(r0, 8)
    here = ref[pl.ds(p0, planes), rows, :]
    lap = 3.0 * STENCIL[0] * here
    for d in range(1, 5):
        pairs = ref[pl.ds(p0 + d, planes), rows, :] + ref[pl.ds(p0 - d, planes), rows, :]
        pairs = pairs + ref[pl.ds(p0, planes), pl.ds(r0 + d, 8), :]
        pairs = pairs + ref[pl.ds(p0, planes), pl.ds(r0 - d, 8), :]
        lap = lap + STENCIL[d] * pairs
        lap = lap + pltpu.roll(here, d, 2) * zmask[2 * d - 2][None]
        lap = lap + pltpu.roll(here, here.shape[2] - d, 2) * zmask[2 * d - 1][None]
    at = (pl.ds(p0, planes), rows)
    return 2.0 * here - prev[at] + courant[at] * lap + pulse * mask[at]


def total_of(parts):
    total = parts[0]
    for k in range(1, parts.shape[0]):
        total = total + parts[k]
    return total


def step_kernel(
    p_now, p_prev, velocity, density, wavelet, source, receivers_in, cells_in, observed_in,
    field, traces, residual, gradient, crossed,
    receivers, cells, observed, small,
    w, v, courant, mask, zmask, hits,
    init_send, init_recv, halo_send, halo_recv, tail_send, tail_recv,
    groups, stations, depth, tiles, sums, low_row, group_send, group_recv,
    models, model_send, model_recv, local,
    record_rows, early_z, early_x, early_y, late_z, late_x, late_y, end_z, end_x, end_y,
    ring_send, ring_recv, corner_out, corner_in, spreading,
):
    slab, block, low, core = place()
    slabs = lax.axis_size(MP)
    blocks = lax.axis_size("station_hi") * 2
    lateral, vertical = p_now.shape[1:]
    same = core == low
    inner = 1 - 2 * core
    outer = -inner
    pair = 1 - 2 * low

    def there(ds, db):
        return (slab + ds >= 0) & (slab + ds < slabs) & (block + db >= 0) & (block + db < blocks)

    def window(b):
        start = jnp.clip(8 * (b - 1), 0, lateral - 24)
        return pl.multiple_of(start, 8), pl.multiple_of(ROW0 + start - 8 * b, 8)

    barrier = pltpu.get_barrier_semaphore()
    for other in range(2 * blocks):
        b, k = other // 2, other % 2

        @pl.when((b != block) | (k != core))
        def _():
            pl.semaphore_signal(
                barrier, 1, device_id=device_at(slab - core + k, b), device_id_type=MESH_ID
            )

    for db in (-1, 0, 1):

        @pl.when(there(outer, db))
        def _():
            pl.semaphore_signal(
                barrier, 1, device_id=device_at(slab + outer, block + db), device_id_type=MESH_ID
            )

    x, z, high = lax.axis_index("x"), lax.axis_index("z"), block // 2
    nx, nz = lax.axis_size("x"), lax.axis_size("z")

    def on_z(k):
        return (x, k, low, high, core)

    def on_x(k):
        return (k // 2, z, low, high, lax.rem(k, 2))

    def on_y(k):
        return device_at(slab, k)

    me_z, me_x, me_y = z, 2 * x + core, block
    for d in range(1, nz):
        pl.semaphore_signal(
            barrier, 1, device_id=on_z(lax.rem(z + d, nz)), device_id_type=MESH_ID
        )
    for d in range(1, nx):
        for k in range(2):
            pl.semaphore_signal(
                barrier, 1, device_id=on_x(2 * lax.rem(x + d, nx) + k), device_id_type=MESH_ID
            )
    kept = (x * nz + z) * 2 + low
    onward = 2 * low - 1
    beyond = kept + onward
    more = (beyond >= 0) & (beyond < slabs)
    far = (beyond // (2 * nz), lax.rem(beyond // 2, nz), 1 - low, high, core)

    @pl.when(more)
    def _():
        pl.semaphore_signal(barrier, 1, device_id=far, device_id_type=MESH_ID)

    smalls = [
        pltpu.make_async_copy(a, b, small.at[n])
        for n, (a, b) in enumerate(
            (
                (cells_in, cells), (observed_in, observed), (receivers_in, receivers),
            )
        )
    ]
    for copy in smalls:
        copy.start()

    start, to = window(block)
    rows = pl.multiple_of(8 * block, 8)
    inside = (pl.ds(1, 8), pl.ds(8, lateral))
    loads = [
        pltpu.make_async_copy(density, models.at[(1, *inside)], local.at[3]),
        pltpu.make_async_copy(velocity, models.at[(0, *inside)], local.at[4]),
    ]
    for copy in loads:
        copy.start()
    inner_left = inner < 0

    def local_copies(own_slab):
        if own_slab:
            pairs_of = [
                (a.at[:, pl.ds(start, 24), :], p.at[pl.ds(PLANE0, 8), pl.ds(to, 24), :])
                for a, p in ((p_now, w.at[0]), (p_prev, v), (velocity, courant))
            ]
        else:
            pairs_of = [
                (
                    p_now.at[:, pl.ds(start, 24), :],
                    w.at[0, pl.ds(jnp.where(inner_left, 0, 16), 8), pl.ds(to, 24), :],
                )
            ] + [
                (
                    a.at[pl.ds(jnp.where(inner_left, 4, 0), 4), pl.ds(rows, 8), :],
                    p.at[pl.ds(jnp.where(inner_left, 4, 16), 4), pl.ds(ROW0, 8), :],
                )
                for a, p in ((p_prev, v), (velocity, courant))
            ]
        return [
            pltpu.make_async_copy(a, b, local.at[n]) for n, (a, b) in enumerate(pairs_of)
        ]

    @pl.when(same)
    def _():
        for copy in local_copies(True):
            copy.start()

    @pl.when(jnp.logical_not(same))
    def _():
        for copy in local_copies(False):
            copy.start()

    def clear(at):
        shape = (at[0].size, at[1].size, vertical)
        for ref in (w.at[0], w.at[1], v, courant):
            ref[at] = jnp.zeros(shape, jnp.float32)

    pl.when(slab == 0)(lambda: clear((pl.ds(0, 8), pl.ds(8, 24))))
    pl.when(slab == slabs - 1)(lambda: clear((pl.ds(16, 8), pl.ds(8, 24))))
    pl.when(block == 0)(lambda: clear((pl.ds(0, 24), pl.ds(8, 8))))
    pl.when(block == blocks - 1)(lambda: clear((pl.ds(0, 24), pl.ds(24, 8))))
    for n in range(2):
        for plane in (0, 9):

            @pl.when(kept == (0 if plane == 0 else slabs - 1))
            def _():
                models[n, plane, pl.ds(8, lateral), :] = jnp.zeros((lateral, vertical), jnp.float32)

        for row in (0, 8 + lateral):
            models[n, :, pl.ds(row, 8), :] = jnp.zeros((10, 8, vertical), jnp.float32)

    crossing = sum(jnp.where(there(outer, db), 1, 0) for db in (-1, 0, 1))
    pl.semaphore_wait(
        barrier, 2 * blocks - 1 + crossing + nz - 1 + 2 * (nx - 1) + jnp.where(more, 1, 0)
    )

    own_group = 2 * high + core
    smalls[0].wait()
    smalls[1].wait()
    sizes = (lateral.bit_length() - 1, lateral - 1)
    groups[own_group, pl.ds(0, 1), :] = (cells[...] >> sizes[0]).astype(jnp.float32)
    groups[own_group, pl.ds(1, 1), :] = (cells[...] & sizes[1]).astype(jnp.float32)
    groups[own_group, pl.ds(2, 1), :] = observed[...]

    def group_copy(d, forth):
        other = lax.rem(own_group + (d if forth else blocks - d), blocks)
        return pltpu.make_async_remote_copy(
            groups.at[own_group], groups.at[own_group if forth else other],
            group_send.at[d], group_recv.at[own_group if forth else other],
            device_id=(x, z, low, other // 2, lax.rem(other, 2)), device_id_type=MESH_ID,
        )

    for d in range(1, blocks):
        group_copy(d, True).start()

    arrays = (p_now, p_prev, velocity)
    places = (w.at[0], v, courant)

    def own_package(n, b, target):
        begin, landing = window(b)
        return pltpu.make_async_remote_copy(
            arrays[n].at[:, pl.ds(begin, 24), :],
            places[n].at[pl.ds(PLANE0, 8), pl.ds(landing, 24), :],
            init_send.at[3, n], init_recv.at[0, n], device_id=target, device_id_type=MESH_ID,
        )

    def halo_package(b, side, target, k, landing):
        begin, to_row = window(b)
        left = side < 0
        near, far_off = jnp.where(left, 4, 0), jnp.where(left, 0, 4)
        near_to, far_to = jnp.where(left, 4, 16), jnp.where(left, 0, 20)
        home = pl.multiple_of(8 * b, 8)
        block_at, block_to = pl.ds(home, 8), pl.ds(ROW0, 8)
        parts = [
            (p_now.at[pl.ds(near, 4), pl.ds(begin, 24), :], w.at[0, pl.ds(near_to, 4), pl.ds(to_row, 24), :]),
            (p_now.at[pl.ds(far_off, 4), block_at, :], w.at[0, pl.ds(far_to, 4), block_to, :]),
        ] + [
            (a.at[pl.ds(near, 4), block_at, :], p.at[pl.ds(near_to, 4), block_to, :])
            for a, p in ((p_prev, v), (velocity, courant))
        ]
        return [
            pltpu.make_async_remote_copy(
                a, p, init_send.at[k, n], init_recv.at[landing, n],
                device_id=target, device_id_type=MESH_ID,
            )
            for n, (a, p) in enumerate(parts)
        ]

    paired = block + pair
    across = lax.rem(block - pair + blocks, blocks)
    partner = device_at(slab, paired)

    @pl.when(same)
    def _():
        own_package(0, paired, partner).start()
        for n in (1, 2):
            own_package(n, across, device_at(slab, across)).start()
        for k, b in ((1, block), (2, paired)):

            @pl.when(there(outer, 0))
            def _():
                for copy in halo_package(b, -outer, device_at(slab + outer, b), k, 2):
                    copy.start()

    @pl.when(jnp.logical_not(same))
    def _():
        for copy in halo_package(paired, inner, partner, 0, 1):
            copy.start()

    def model_copy(n, outward, forth):
        e = onward if outward else -onward
        if forth:
            plane, landing = jnp.where(e > 0, 7, 0), jnp.where(e > 0, 0, 9)
        else:
            plane, landing = 0, jnp.where(e > 0, 9, 0)
        k = 1 if outward else 0
        return pltpu.make_async_remote_copy(
            (velocity, density)[n].at[plane], models.at[n, landing, pl.ds(8, lateral), :],
            model_send.at[n, k], model_recv.at[n, k],
            device_id=far if outward else partner, device_id_type=MESH_ID,
        )

    for copy in smalls[2:]:
        copy.wait()
    source_cell = source[0]
    source_z = lax.rem(source_cell, vertical)
    source_xy = source_cell // vertical
    source_y = lax.rem(source_xy, lateral)
    source_x = source_xy // lateral
    shape = (24, 24, vertical)
    at_x = lax.broadcasted_iota(jnp.int32, shape, 0) + (8 * slab - PLANE0)
    at_y = lax.broadcasted_iota(jnp.int32, shape, 1) + (8 * block + 8 - ROW0)
    at_z = lax.broadcasted_iota(jnp.int32, shape, 2)
    hit = (at_x == source_x) & (at_y == source_y) & (at_z == source_z)
    mask[:, pl.ds(8, 24), :] = jnp.where(hit, 1.0, 0.0)
    lane = lax.broadcasted_iota(jnp.int32, (8, vertical), 1)
    for d in range(1, 5):
        zmask[2 * d - 2] = jnp.where(lane >= d, STENCIL[d], 0.0)
        zmask[2 * d - 1] = jnp.where(lane < vertical - d, STENCIL[d], 0.0)
    nrec = receivers.shape[1]
    cell = (8 * slab + lax.broadcasted_iota(jnp.int32, (8, 8, nrec), 0)) * lateral + (
        8 * block + lax.broadcasted_iota(jnp.int32, (8, 8, nrec), 1)
    )
    hits[...] = jnp.where(cell == receivers[...][None], 1.0, 0.0)

    step_z = lax.broadcasted_iota(jnp.int32, (vertical, 128), 0).astype(jnp.float32) + 1.0
    depth[0] = step_z
    depth[1] = step_z * step_z
    share = pl.multiple_of(8 * own_group, 8)
    ngroups = groups.shape[0]
    sums[...] = jnp.zeros(sums.shape, jnp.float32)
    record_rows[3] = jnp.zeros((8, 128), jnp.float32)
    eye = lax.broadcasted_iota(jnp.int32, (128, 128), 0) == lax.broadcasted_iota(
        jnp.int32, (128, 128), 1
    )

    def column(row):
        picked = jnp.where(eye, jnp.broadcast_to(row, (128, 128)), 0.0).astype(jnp.bfloat16)
        ones = jnp.ones((128, 128), jnp.bfloat16)
        return jnp.dot(picked, ones, preferred_element_type=jnp.float32)

    def forward(q, unused):
        p, r = q // 4, 2 * lax.rem(q, 4)
        dx = (8 * kept + p).astype(jnp.float32) - stations[0]
        for u in range(2):
            dy = (share + r + u).astype(jnp.float32) - stations[1]
            flat = dx * dx + dy * dy
            weight = column(models[1, p + 1, pl.ds(8 + share + r + u, 1), :])
            for g in range(ngroups):
                inverse = lax.rsqrt(flat[g : g + 1, :] + depth[1])
                tile = ((depth[0] * inverse) * (inverse * inverse)).astype(jnp.bfloat16)
                tiles[q, pl.ds(u * vertical, vertical), pl.ds(g * 128, 128)] = tile
                part = tile.astype(jnp.float32) * weight
                sums[g] += jnp.sum(part.reshape(vertical // 8, 8, 128), axis=0)
        return unused

    def adjoint(p, unused):
        each = tiles.shape[0] // 8
        slab_tiles = tiles[pl.ds(p * each, each)].reshape(each * 2 * vertical, ngroups * 128)
        out = jnp.dot(slab_tiles, spreading[...], preferred_element_type=jnp.float32)
        for r in range(2 * each):
            unit = jnp.where(eye, out[vertical * r : vertical * (r + 1)], 0.0)
            part = jnp.sum(unit.reshape(vertical // 8, 8, 128), axis=0)
            gradient[p, pl.ds(r, 1), :] = jnp.sum(part, axis=0, keepdims=True)
        return unused

    def cross_plane(p, unused):
        lanes = lax.broadcasted_iota(jnp.int32, (lateral, vertical), 1)

        def slopes(f):
            mid = f[p + 1, pl.ds(8, lateral), :]
            along_x = (f[p + 2, pl.ds(8, lateral), :] - f[p, pl.ds(8, lateral), :]) * 0.5
            along_y = (f[p + 1, pl.ds(9, lateral), :] - f[p + 1, pl.ds(7, lateral), :]) * 0.5
            after = jnp.where(lanes < vertical - 1, pltpu.roll(mid, vertical - 1, 1), 0.0)
            before = jnp.where(lanes > 0, pltpu.roll(mid, 1, 1), 0.0)
            return along_x, along_y, (after - before) * 0.5

        vx, vy, vz = slopes(models.at[0])
        qx, qy, qz = slopes(models.at[1])
        crossed[0, p] = vy * qz - vz * qy
        crossed[1, p] = vz * qx - vx * qz
        crossed[2, p] = vx * qy - vy * qx
        return unused

    loads[0].wait()
    for d in range(1, blocks):
        group_copy(d, True).wait_send()
        group_copy(d, False).wait_recv()
    for g in range(ngroups):
        for n in range(3):
            stations[n, pl.ds(g, 1), :] = groups[g, pl.ds(n, 1), :]
    pairs_all = tiles.shape[0]
    share_of = pairs_all * 3 // 16
    lax.fori_loop(0, share_of, forward, 0)

    @pl.when(same)
    def _():
        own_package(0, paired, partner).wait_send()
        for n in (1, 2):
            own_package(n, across, device_at(slab, across)).wait_send()
        for k, b in ((1, block), (2, paired)):

            @pl.when(there(outer, 0))
            def _():
                for copy in halo_package(b, -outer, device_at(slab + outer, b), k, 2):
                    copy.wait_send()

        for copy in halo_package(block, inner, partner, 0, 1):
            copy.wait_recv()
        for copy in local_copies(True):
            copy.wait()

    @pl.when(jnp.logical_not(same))
    def _():
        for copy in halo_package(paired, inner, partner, 0, 1):
            copy.wait_send()
        for n in range(3):
            own_package(n, block, partner).wait_recv()
        for copy in local_copies(False):
            copy.wait()

    @pl.when(there(outer, 0))
    def _():
        for copy in halo_package(block, outer, partner, 0, 2):
            copy.wait_recv()

    scaled = TIME_RATIO * courant[:, pl.ds(8, 24), :]
    courant[:, pl.ds(8, 24), :] = scaled * scaled

    order = (4, 5, 6, 7, 2, 3, 0, 1)

    def halo(slot, k, forth):
        ds, db = SIDES[k]
        opposite = SIDES.index((-ds, -db))
        if k >= 4:
            begin = corner_out.at[k - 4]
            end = corner_in.at[slot, (opposite if forth else k) - 4]
        else:
            begin = w.at[slot, pl.ds(PLANE0, 8), pl.ds(ROW0, 8), :]
            sign = -1 if forth else 1
            end = w.at[
                slot, pl.ds(PLANE0 + 8 * sign * ds, 8), pl.ds(ROW0 + 8 * sign * db, 8), :
            ]
        return pltpu.make_async_remote_copy(
            begin, end, halo_send.at[k], halo_recv.at[slot, opposite if forth else k],
            device_id=device_at(slab + ds, block + db), device_id_type=MESH_ID,
        )

    def corner_rows(k, outside):
        ds, db = SIDES[k]
        plane = (16 if ds > 0 else 4) if outside else (12 if ds > 0 else 8)
        row = (24 if db > 0 else 12) if outside else (20 if db > 0 else 16)
        return plane, row

    def stage_corner(slot, k):
        plane, row = corner_rows(k, False)
        for n in range(4):
            corner_out[k - 4, n // 2, pl.ds(4 * (n % 2), 4), :] = w[slot, plane + n, pl.ds(row, 4), :]

    def place_corner(slot, k):
        plane, row = corner_rows(k, True)
        for n in range(4):
            w[slot, plane + n, pl.ds(row, 4), :] = corner_in[slot, k - 4, n // 2, pl.ds(4 * (n % 2), 4), :]

    own = (pl.ds(PLANE0, 8), pl.ds(ROW0, 8))

    def record(values, n):
        top = jnp.broadcast_to(values[:, :, 0:1], values.shape)
        for half in range(nrec // 128):
            part = jnp.sum(top * hits[:, :, half * 128 : (half + 1) * 128], axis=0)
            row = n * (nrec // 128) + half
            record_rows[row // 8, pl.ds(lax.rem(row, 8), 1), :] = jnp.sum(part, axis=0, keepdims=True)

    def first(slot, m):
        pulse = wavelet[2 * m]
        here = w.at[slot]
        for p0 in (4, 16):
            new = advance(here, v, courant, mask, pulse, zmask, p0, 4, ROW0)
            v[pl.ds(p0, 4), pl.ds(ROW0, 8), :] = new
        for p0 in range(8, 16, 2):
            for r0 in (12, 20):
                new = advance(here, v, courant, mask, pulse, zmask, p0, 2, r0)
                v[pl.ds(p0, 2), pl.ds(r0, 8), :] = new

    def second(slot, m, target):
        pulse = wavelet[2 * m + 1]
        for p0 in range(8, 16, 2):
            new = advance(v, w.at[slot], courant, mask, pulse, zmask, p0, 2, ROW0)
            target[pl.ds(p0, 2), pl.ds(ROW0, 8), :] = new

    pairs = wavelet.shape[0] // 2

    def ring(k, buffer, me, n, address, forth, d):
        other = lax.rem(me + (d if forth else n - d), n)
        return pltpu.make_async_remote_copy(
            buffer.at[me], buffer.at[me if forth else other],
            ring_send.at[k, d], ring_recv.at[k, me if forth else other],
            device_id=address(other), device_id_type=MESH_ID,
        )

    def spread(k, buffer, me, address):
        for d in range(1, buffer.shape[0]):
            ring(k, buffer, me, buffer.shape[0], address, True, d).start()

    def gathered(k, buffer, me, address):
        for d in range(1, buffer.shape[0]):
            ring(k, buffer, me, buffer.shape[0], address, True, d).wait_send()
            ring(k, buffer, me, buffer.shape[0], address, False, d).wait_recv()
        return total_of(buffer)

    def step(m, background):
        slot = lax.rem(m, 2)
        later = 1 - slot
        first(slot, m)
        second(slot, m, w.at[later])
        for k in range(4, 8):
            stage_corner(later, k)
        for k in order:

            @pl.when(there(*SIDES[k]))
            def _():
                halo(later, k, True).start()

        record(v[own], 2 * m)
        record(w[(later, *own)], 2 * m + 1)
        background()
        for k in (0, 1, 2, 3, 4, 5, 6, 7):

            @pl.when(there(*SIDES[k]))
            def _():
                halo(later, k, True).wait_send()
                halo(later, k, False).wait_recv()
                if k >= 4:
                    place_corner(later, k)

    def model_ways():
        for n in range(2):
            for outward in (False, True):
                yield n, outward, (more if outward else more | True)

    def body(m, unused):
        def background():
            @pl.when(m == 1)
            def _():
                for n, outward, really in model_ways():

                    @pl.when(really)
                    def _():
                        model_copy(n, outward, True).start()

            lax.fori_loop(share_of * (m + 1), share_of * (m + 2), forward, 0)

        step(m, background)
        return unused

    lax.fori_loop(0, 4, body, 0)

    def background_4():
        lax.fori_loop(share_of * 5, pairs_all, forward, 0)
        for g in range(ngroups):
            early_z[me_z, 0, pl.ds(g, 1), :] = jnp.sum(sums[g], axis=0, keepdims=True)
        early_z[me_z, 1] = record_rows[0]
        early_z[me_z, 2] = record_rows[1]
        spread(0, early_z, me_z, on_z)

    def background_5():
        loads[1].wait()
        for n, outward, really in model_ways():

            @pl.when(really)
            def _():
                model_copy(n, outward, True).wait_send()
                model_copy(n, outward, False).wait_recv()

        lax.fori_loop(0, 8, cross_plane, 0)

    def background_6():
        late_z[me_z, 0] = record_rows[2]
        late_z[me_z, 1] = record_rows[3]
        early_x[me_x] = gathered(0, early_z, me_z, on_z)
        spread(1, early_x, me_x, on_x)
        spread(3, late_z, me_z, on_z)

    def put_traces(rows_at, first_step, count):
        for n in range(count):
            for half in range(2):
                traces[pl.ds(first_step + n, 1), pl.ds(128 * half, 128)] = rows_at[
                    2 * n + half : 2 * n + half + 1, :
                ]

    step(4, background_4)
    step(5, background_5)
    step(6, background_6)
    slot = (pairs - 1) % 2
    first(slot, pairs - 1)
    second(slot, pairs - 1, w.at[1 - slot])
    last = w.at[1 - slot]

    def handing(to, k):
        return pltpu.make_async_remote_copy(
            last.at[own], field.at[:, pl.ds(rows, 8), :],
            tail_send.at[to, k], tail_recv.at[block],
            device_id=(*device_at(slab, 2 * to + core)[:4], k), device_id_type=MESH_ID,
        )

    for to in range(blocks // 2):
        for k in range(2):

            @pl.when((2 * to + core != block) | (k != core))
            def _():
                handing(to, k).start()

    @pl.when(same)
    def _():
        field[:, pl.ds(rows, 8), :] = last[own]

    record(v[own], 2 * pairs - 2)
    record(last[own], 2 * pairs - 1)
    end_z[me_z] = record_rows[3, pl.ds(4, 4), :]
    spread(6, end_z, me_z, on_z)
    early_y[me_y] = gathered(1, early_x, me_x, on_x)
    spread(2, early_y, me_y, on_y)
    late_x[me_x] = gathered(3, late_z, me_z, on_z)
    spread(4, late_x, me_x, on_x)
    total = gathered(2, early_y, me_y, on_y)
    left_over = total[0, :ngroups] - stations[2]
    stations[0] = left_over
    residual[...] = stations[0, pl.ds(own_group, 1), :]
    for g in range(ngroups):
        spreading[pl.ds(128 * g, 128), :] = column(left_over[g : g + 1, :]).astype(jnp.bfloat16)
    put_traces(total[1], 0, 4)
    put_traces(total[2], 4, 4)
    end_x[me_x] = gathered(6, end_z, me_z, on_z)
    spread(7, end_x, me_x, on_x)
    late_y[me_y] = gathered(4, late_x, me_x, on_x)
    spread(5, late_y, me_y, on_y)
    lax.fori_loop(0, 4, adjoint, 0)
    end_y[me_y] = gathered(7, end_x, me_x, on_x)
    spread(8, end_y, me_y, on_y)
    lax.fori_loop(4, 8, adjoint, 0)
    total = gathered(5, late_y, me_y, on_y)
    put_traces(total[0], 8, 4)
    put_traces(total[1], 12, 2)
    put_traces(gathered(8, end_y, me_y, on_y), 14, 2)
    for to in range(blocks // 2):
        for k in range(2):

            @pl.when((2 * to + core != block) | (k != core))
            def _():
                handing(to, k).wait_send()

    for b in range(blocks):

        @pl.when((b != block) | jnp.logical_not(same))
        def _():
            pltpu.make_async_remote_copy(
                last.at[own], field.at[:, pl.ds(8 * b, 8), :],
                tail_send.at[0, 0], tail_recv.at[b],
                device_id=partner, device_id_type=MESH_ID,
            ).wait_recv()


def store_kernel(*refs):
    copies = [pltpu.make_async_copy(refs[n], refs[5 + n], refs[10].at[n]) for n in range(5)]
    for copy in copies:
        copy.start()
    for copy in copies:
        copy.wait()


def in_hbm(array):
    return pltpu.with_memory_space_constraint(array, pltpu.HBM)


def per_device(
    p_now, p_prev, velocity, density, wavelet, source_cell, receiver_cells, station_cells, observed
):
    planes, lateral, vertical = p_now.shape
    nrec = receiver_cells.shape[0]
    blocks = lax.axis_size("station_hi") * 2
    nx, nz = lax.axis_size("x"), lax.axis_size("z")
    group = station_cells.shape[0]
    f32 = jnp.float32
    padded = (24, 40, vertical)
    vmem, smem = (pl.BlockSpec(memory_space=space) for space in (pltpu.VMEM, pltpu.SMEM))
    hbm = pl.BlockSpec(memory_space=pltpu.HBM)
    dma = pltpu.SemaphoreType.DMA
    longest = max(nz, 2 * nx, blocks)
    results = pl.pallas_call(
        step_kernel,
        out_shape=(
            jax.ShapeDtypeStruct(p_now.shape, f32),
            jax.ShapeDtypeStruct((wavelet.shape[0], nrec), f32),
            jax.ShapeDtypeStruct((1, group), f32),
            jax.ShapeDtypeStruct((planes, lateral // blocks, vertical), f32),
            jax.ShapeDtypeStruct((3, *p_now.shape), f32),
        ),
        in_specs=[hbm] * 4 + [smem] * 2 + [hbm] * 3,
        out_specs=(vmem,) * 5,
        scratch_shapes=[
            pltpu.VMEM((1, nrec), jnp.int32), pltpu.VMEM((1, group), jnp.int32),
            pltpu.VMEM((1, group), f32), dma((3,)),
            pltpu.VMEM((2, *padded), f32),
            pltpu.VMEM(padded, f32),
            pltpu.VMEM(padded, f32),
            pltpu.VMEM(padded, f32),
            pltpu.VMEM((8, 8, vertical), f32),
            pltpu.VMEM((8, 8, nrec), f32),
            dma((4, 4)), dma((3, 4)), dma((8,)), dma((2, 8)), dma((blocks // 2, 2)), dma((blocks,)),
            pltpu.VMEM((blocks, 8, group), f32),
            pltpu.VMEM((3, blocks, group), f32),
            pltpu.VMEM((2, vertical, 128), f32),
            pltpu.VMEM((planes * 4, 2 * vertical, blocks * group), jnp.bfloat16),
            pltpu.VMEM((blocks, 8, group), f32),
            pltpu.VMEM((1, blocks * group), f32),
            dma((blocks,)), dma((blocks,)),
            pltpu.VMEM((2, planes + 2, lateral + 16, vertical), f32),
            dma((2, 2)), dma((2, 2)), dma((5,)),
            pltpu.VMEM((4, 8, 128), f32),
            *(pltpu.VMEM((n, 3, 8, 128), f32) for n in (nz, 2 * nx, blocks)),
            *(pltpu.VMEM((n, 2, 8, 128), f32) for n in (nz, 2 * nx, blocks)),
            *(pltpu.VMEM((n, 4, 128), f32) for n in (nz, 2 * nx, blocks)),
            dma((9, longest)), dma((9, longest)),
            pltpu.VMEM((4, 2, 8, vertical), f32),
            pltpu.VMEM((2, 4, 2, 8, vertical), f32),
            pltpu.VMEM((blocks * group, 128), jnp.bfloat16),
        ],
        compiler_params=pltpu.CompilerParams(
            collective_id=0, has_side_effects=True, vmem_limit_bytes=48 * 2**20
        ),
    )(
        *map(in_hbm, (p_now, p_prev, velocity, density)), wavelet, source_cell,
        *(in_hbm(a.reshape(1, -1)) for a in (receiver_cells, station_cells, observed)),
    )
    field, traces, residual, gradient, crossed = pl.pallas_call(
        store_kernel,
        out_shape=tuple(jax.ShapeDtypeStruct(r.shape, r.dtype) for r in results),
        in_specs=[vmem] * 5,
        out_specs=(hbm,) * 5,
        scratch_shapes=[dma((5,))],
        compiler_params=pltpu.CompilerParams(vmem_limit_bytes=2 * 2**20),
    )(*results)
    return field, traces, residual.reshape(-1), gradient, crossed


def solution(mesh):
    split = Mesh(mesh.devices.reshape(*SPLIT, mesh.shape["station"] // 2, 2), MESH)
    slabs = P(MP, None, None)
    return jax.shard_map(
        per_device,
        mesh=split,
        in_specs=(slabs, slabs, slabs, slabs, P(), P(), P(), P(STATION), P(STATION)),
        out_specs=(slabs, P(), P(STATION), P(MP, STATION, None), P(None, MP, None, None)),
        check_vma=False,
    )
```

```python
import jax
import jax.numpy as jnp
from jax import lax
from jax.experimental import pallas as pl
from jax.experimental.pallas import tpu as pltpu
from jax.sharding import Mesh
from jax.sharding import PartitionSpec as P

MP = ("x", "z", "y_lo")
STATION = ("station_hi", "core")
MESH = MP + STATION
SPLIT = (4, 12, 2)
STENCIL = (-205.0 / 72.0, 8.0 / 5.0, -1.0 / 5.0, 8.0 / 315.0, -1.0 / 560.0)
TIME_RATIO = 0.1
MESH_ID = pl.DeviceIdType.MESH
SIDES = ((-1, 0), (1, 0), (0, -1), (0, 1), (-1, -1), (-1, 1), (1, -1), (1, 1))
ROW0 = 16
PLANE0 = 8


def place():
    x, z, low, high, core = (lax.axis_index(axis) for axis in MESH)
    nz = lax.axis_size("z")
    slab = (x * nz + z) * 2 + core
    return slab, high * 2 + low, low, core


def device_at(slab, block):
    nz = lax.axis_size("z")
    column = slab // 2
    return (column // nz, lax.rem(column, nz), lax.rem(block, 2), block // 2, lax.rem(slab, 2))


def advance(ref, prev, courant, mask, pulse, zmask, p0, planes, r0):
    rows = pl.ds(r0, 8)
    here = ref[pl.ds(p0, planes), rows, :]
    lap = 3.0 * STENCIL[0] * here
    for d in range(1, 5):
        pairs = ref[pl.ds(p0 + d, planes), rows, :] + ref[pl.ds(p0 - d, planes), rows, :]
        pairs = pairs + ref[pl.ds(p0, planes), pl.ds(r0 + d, 8), :]
        pairs = pairs + ref[pl.ds(p0, planes), pl.ds(r0 - d, 8), :]
        lap = lap + STENCIL[d] * pairs
        lap = lap + pltpu.roll(here, d, 2) * zmask[2 * d - 2][None]
        lap = lap + pltpu.roll(here, here.shape[2] - d, 2) * zmask[2 * d - 1][None]
    at = (pl.ds(p0, planes), rows)
    return 2.0 * here - prev[at] + courant[at] * lap + pulse * mask[at]


def total_of(parts):
    total = parts[0]
    for k in range(1, parts.shape[0]):
        total = total + parts[k]
    return total


def step_kernel(
    p_now, p_prev, velocity, density, wavelet, source, receivers_in, cells_in, observed_in,
    field, traces, residual, gradient, crossed,
    receivers, cells, observed, small,
    w, v, courant, mask, zmask, hits,
    init_send, init_recv, halo_send, halo_recv, tail_send, tail_recv,
    groups, stations, depth, tiles, sums, low_row, group_send, group_recv,
    models, model_send, model_recv, local,
    record_rows, early_z, early_x, early_y, late_z, late_x, late_y, end_z,
    ring_send, ring_recv, corner_out, corner_in, spreading,
):
    slab, block, low, core = place()
    slabs = lax.axis_size(MP)
    blocks = lax.axis_size("station_hi") * 2
    lateral, vertical = p_now.shape[1:]
    same = core == low
    inner = 1 - 2 * core
    outer = -inner
    pair = 1 - 2 * low

    def there(ds, db):
        return (slab + ds >= 0) & (slab + ds < slabs) & (block + db >= 0) & (block + db < blocks)

    def window(b):
        start = jnp.clip(8 * (b - 1), 0, lateral - 24)
        return pl.multiple_of(start, 8), pl.multiple_of(ROW0 + start - 8 * b, 8)

    barrier = pltpu.get_barrier_semaphore()
    for other in range(2 * blocks):
        b, k = other // 2, other % 2

        @pl.when((b != block) | (k != core))
        def _():
            pl.semaphore_signal(
                barrier, 1, device_id=device_at(slab - core + k, b), device_id_type=MESH_ID
            )

    for db in (-1, 0, 1):

        @pl.when(there(outer, db))
        def _():
            pl.semaphore_signal(
                barrier, 1, device_id=device_at(slab + outer, block + db), device_id_type=MESH_ID
            )

    x, z, high = lax.axis_index("x"), lax.axis_index("z"), block // 2
    nx, nz = lax.axis_size("x"), lax.axis_size("z")

    def on_z(k):
        return (x, k, low, high, core)

    def on_x(k):
        return (k // 2, z, low, high, lax.rem(k, 2))

    def on_y(k):
        return device_at(slab, k)

    me_z, me_x, me_y = z, 2 * x + core, block
    for d in range(1, nz):
        pl.semaphore_signal(
            barrier, 1, device_id=on_z(lax.rem(z + d, nz)), device_id_type=MESH_ID
        )
    for d in range(1, nx):
        for k in range(2):
            pl.semaphore_signal(
                barrier, 1, device_id=on_x(2 * lax.rem(x + d, nx) + k), device_id_type=MESH_ID
            )
    kept = (x * nz + z) * 2 + low
    onward = 2 * low - 1
    beyond = kept + onward
    more = (beyond >= 0) & (beyond < slabs)
    far = (beyond // (2 * nz), lax.rem(beyond // 2, nz), 1 - low, high, core)

    @pl.when(more)
    def _():
        pl.semaphore_signal(barrier, 1, device_id=far, device_id_type=MESH_ID)

    smalls = [
        pltpu.make_async_copy(a, b, small.at[n])
        for n, (a, b) in enumerate(
            (
                (cells_in, cells), (observed_in, observed), (receivers_in, receivers),
            )
        )
    ]
    for copy in smalls:
        copy.start()

    start, to = window(block)
    rows = pl.multiple_of(8 * block, 8)
    inside = (pl.ds(1, 8), pl.ds(8, lateral))
    loads = [
        pltpu.make_async_copy(density, models.at[(1, *inside)], local.at[3]),
        pltpu.make_async_copy(velocity, models.at[(0, *inside)], local.at[4]),
    ]
    for copy in loads:
        copy.start()
    inner_left = inner < 0

    def local_copies(own_slab):
        if own_slab:
            pairs_of = [
                (a.at[:, pl.ds(start, 24), :], p.at[pl.ds(PLANE0, 8), pl.ds(to, 24), :])
                for a, p in ((p_now, w.at[0]), (p_prev, v), (velocity, courant))
            ]
        else:
            pairs_of = [
                (
                    p_now.at[:, pl.ds(start, 24), :],
                    w.at[0, pl.ds(jnp.where(inner_left, 0, 16), 8), pl.ds(to, 24), :],
                )
            ] + [
                (
                    a.at[pl.ds(jnp.where(inner_left, 4, 0), 4), pl.ds(rows, 8), :],
                    p.at[pl.ds(jnp.where(inner_left, 4, 16), 4), pl.ds(ROW0, 8), :],
                )
                for a, p in ((p_prev, v), (velocity, courant))
            ]
        return [
            pltpu.make_async_copy(a, b, local.at[n]) for n, (a, b) in enumerate(pairs_of)
        ]

    @pl.when(same)
    def _():
        for copy in local_copies(True):
            copy.start()

    @pl.when(jnp.logical_not(same))
    def _():
        for copy in local_copies(False):
            copy.start()

    def clear(at):
        shape = (at[0].size, at[1].size, vertical)
        for ref in (w.at[0], w.at[1], v, courant):
            ref[at] = jnp.zeros(shape, jnp.float32)

    pl.when(slab == 0)(lambda: clear((pl.ds(0, 8), pl.ds(8, 24))))
    pl.when(slab == slabs - 1)(lambda: clear((pl.ds(16, 8), pl.ds(8, 24))))
    pl.when(block == 0)(lambda: clear((pl.ds(0, 24), pl.ds(8, 8))))
    pl.when(block == blocks - 1)(lambda: clear((pl.ds(0, 24), pl.ds(24, 8))))
    for n in range(2):
        for plane in (0, 9):

            @pl.when(kept == (0 if plane == 0 else slabs - 1))
            def _():
                models[n, plane, pl.ds(8, lateral), :] = jnp.zeros((lateral, vertical), jnp.float32)

        for row in (0, 8 + lateral):
            models[n, :, pl.ds(row, 8), :] = jnp.zeros((10, 8, vertical), jnp.float32)

    crossing = sum(jnp.where(there(outer, db), 1, 0) for db in (-1, 0, 1))
    pl.semaphore_wait(
        barrier, 2 * blocks - 1 + crossing + nz - 1 + 2 * (nx - 1) + jnp.where(more, 1, 0)
    )

    own_group = 2 * high + core
    smalls[0].wait()
    smalls[1].wait()
    sizes = (lateral.bit_length() - 1, lateral - 1)
    groups[own_group, pl.ds(0, 1), :] = (cells[...] >> sizes[0]).astype(jnp.float32)
    groups[own_group, pl.ds(1, 1), :] = (cells[...] & sizes[1]).astype(jnp.float32)
    groups[own_group, pl.ds(2, 1), :] = observed[...]

    def group_copy(d, forth):
        other = lax.rem(own_group + (d if forth else blocks - d), blocks)
        return pltpu.make_async_remote_copy(
            groups.at[own_group], groups.at[own_group if forth else other],
            group_send.at[d], group_recv.at[own_group if forth else other],
            device_id=(x, z, low, other // 2, lax.rem(other, 2)), device_id_type=MESH_ID,
        )

    for d in range(1, blocks):
        group_copy(d, True).start()

    arrays = (p_now, p_prev, velocity)
    places = (w.at[0], v, courant)

    def own_package(n, b, target):
        begin, landing = window(b)
        return pltpu.make_async_remote_copy(
            arrays[n].at[:, pl.ds(begin, 24), :],
            places[n].at[pl.ds(PLANE0, 8), pl.ds(landing, 24), :],
            init_send.at[3, n], init_recv.at[0, n], device_id=target, device_id_type=MESH_ID,
        )

    def halo_package(b, side, target, k, landing):
        begin, to_row = window(b)
        left = side < 0
        near, far_off = jnp.where(left, 4, 0), jnp.where(left, 0, 4)
        near_to, far_to = jnp.where(left, 4, 16), jnp.where(left, 0, 20)
        home = pl.multiple_of(8 * b, 8)
        block_at, block_to = pl.ds(home, 8), pl.ds(ROW0, 8)
        parts = [
            (p_now.at[pl.ds(near, 4), pl.ds(begin, 24), :], w.at[0, pl.ds(near_to, 4), pl.ds(to_row, 24), :]),
            (p_now.at[pl.ds(far_off, 4), block_at, :], w.at[0, pl.ds(far_to, 4), block_to, :]),
        ] + [
            (a.at[pl.ds(near, 4), block_at, :], p.at[pl.ds(near_to, 4), block_to, :])
            for a, p in ((p_prev, v), (velocity, courant))
        ]
        return [
            pltpu.make_async_remote_copy(
                a, p, init_send.at[k, n], init_recv.at[landing, n],
                device_id=target, device_id_type=MESH_ID,
            )
            for n, (a, p) in enumerate(parts)
        ]

    paired = block + pair
    across = lax.rem(block - pair + blocks, blocks)
    partner = device_at(slab, paired)

    @pl.when(same)
    def _():
        own_package(0, paired, partner).start()
        for n in (1, 2):
            own_package(n, across, device_at(slab, across)).start()
        for k, b in ((1, block), (2, paired)):

            @pl.when(there(outer, 0))
            def _():
                for copy in halo_package(b, -outer, device_at(slab + outer, b), k, 2):
                    copy.start()

    @pl.when(jnp.logical_not(same))
    def _():
        for copy in halo_package(paired, inner, partner, 0, 1):
            copy.start()

    def model_copy(n, outward, forth):
        e = onward if outward else -onward
        if forth:
            plane, landing = jnp.where(e > 0, 7, 0), jnp.where(e > 0, 0, 9)
        else:
            plane, landing = 0, jnp.where(e > 0, 9, 0)
        k = 1 if outward else 0
        return pltpu.make_async_remote_copy(
            (velocity, density)[n].at[plane], models.at[n, landing, pl.ds(8, lateral), :],
            model_send.at[n, k], model_recv.at[n, k],
            device_id=far if outward else partner, device_id_type=MESH_ID,
        )

    for copy in smalls[2:]:
        copy.wait()
    source_cell = source[0]
    source_z = lax.rem(source_cell, vertical)
    source_xy = source_cell // vertical
    source_y = lax.rem(source_xy, lateral)
    source_x = source_xy // lateral
    shape = (24, 24, vertical)
    at_x = lax.broadcasted_iota(jnp.int32, shape, 0) + (8 * slab - PLANE0)
    at_y = lax.broadcasted_iota(jnp.int32, shape, 1) + (8 * block + 8 - ROW0)
    at_z = lax.broadcasted_iota(jnp.int32, shape, 2)
    hit = (at_x == source_x) & (at_y == source_y) & (at_z == source_z)
    mask[:, pl.ds(8, 24), :] = jnp.where(hit, 1.0, 0.0)
    lane = lax.broadcasted_iota(jnp.int32, (8, vertical), 1)
    for d in range(1, 5):
        zmask[2 * d - 2] = jnp.where(lane >= d, STENCIL[d], 0.0)
        zmask[2 * d - 1] = jnp.where(lane < vertical - d, STENCIL[d], 0.0)
    nrec = receivers.shape[1]
    cell = (8 * slab + lax.broadcasted_iota(jnp.int32, (8, 8, nrec), 0)) * lateral + (
        8 * block + lax.broadcasted_iota(jnp.int32, (8, 8, nrec), 1)
    )
    hits[...] = jnp.where(cell == receivers[...][None], 1.0, 0.0)

    step_z = lax.broadcasted_iota(jnp.int32, (vertical, 128), 0).astype(jnp.float32) + 1.0
    depth[0] = step_z
    depth[1] = step_z * step_z
    share = pl.multiple_of(8 * own_group, 8)
    ngroups = groups.shape[0]
    sums[...] = jnp.zeros(sums.shape, jnp.float32)
    record_rows[3] = jnp.zeros((8, 128), jnp.float32)
    eye = lax.broadcasted_iota(jnp.int32, (128, 128), 0) == lax.broadcasted_iota(
        jnp.int32, (128, 128), 1
    )

    def column(row):
        picked = jnp.where(eye, jnp.broadcast_to(row, (128, 128)), 0.0).astype(jnp.bfloat16)
        ones = jnp.ones((128, 128), jnp.bfloat16)
        return jnp.dot(picked, ones, preferred_element_type=jnp.float32)

    def forward(q, unused):
        p, r = q // 4, 2 * lax.rem(q, 4)
        dx = (8 * kept + p).astype(jnp.float32) - stations[0]
        for u in range(2):
            dy = (share + r + u).astype(jnp.float32) - stations[1]
            flat = dx * dx + dy * dy
            weight = column(models[1, p + 1, pl.ds(8 + share + r + u, 1), :])
            for g in range(ngroups):
                inverse = lax.rsqrt(flat[g : g + 1, :] + depth[1])
                tile = ((depth[0] * inverse) * (inverse * inverse)).astype(jnp.bfloat16)
                tiles[q, pl.ds(u * vertical, vertical), pl.ds(g * 128, 128)] = tile
                part = tile.astype(jnp.float32) * weight
                sums[g] += jnp.sum(part.reshape(vertical // 8, 8, 128), axis=0)
        return unused

    def adjoint(p, unused):
        each = tiles.shape[0] // 8
        slab_tiles = tiles[pl.ds(p * each, each)].reshape(each * 2 * vertical, ngroups * 128)
        out = jnp.dot(slab_tiles, spreading[...], preferred_element_type=jnp.float32)
        for r in range(2 * each):
            unit = jnp.where(eye, out[vertical * r : vertical * (r + 1)], 0.0)
            part = jnp.sum(unit.reshape(vertical // 8, 8, 128), axis=0)
            gradient[p, pl.ds(r, 1), :] = jnp.sum(part, axis=0, keepdims=True)
        return unused

    def cross_plane(p, unused):
        lanes = lax.broadcasted_iota(jnp.int32, (lateral, vertical), 1)

        def slopes(f):
            mid = f[p + 1, pl.ds(8, lateral), :]
            along_x = (f[p + 2, pl.ds(8, lateral), :] - f[p, pl.ds(8, lateral), :]) * 0.5
            along_y = (f[p + 1, pl.ds(9, lateral), :] - f[p + 1, pl.ds(7, lateral), :]) * 0.5
            after = jnp.where(lanes < vertical - 1, pltpu.roll(mid, vertical - 1, 1), 0.0)
            before = jnp.where(lanes > 0, pltpu.roll(mid, 1, 1), 0.0)
            return along_x, along_y, (after - before) * 0.5

        vx, vy, vz = slopes(models.at[0])
        qx, qy, qz = slopes(models.at[1])
        crossed[0, p] = vy * qz - vz * qy
        crossed[1, p] = vz * qx - vx * qz
        crossed[2, p] = vx * qy - vy * qx
        return unused

    loads[0].wait()
    for d in range(1, blocks):
        group_copy(d, True).wait_send()
        group_copy(d, False).wait_recv()
    for g in range(ngroups):
        for n in range(3):
            stations[n, pl.ds(g, 1), :] = groups[g, pl.ds(n, 1), :]
    pairs_all = tiles.shape[0]
    share_of = pairs_all // 4
    lax.fori_loop(0, share_of, forward, 0)

    @pl.when(same)
    def _():
        own_package(0, paired, partner).wait_send()
        for n in (1, 2):
            own_package(n, across, device_at(slab, across)).wait_send()
        for k, b in ((1, block), (2, paired)):

            @pl.when(there(outer, 0))
            def _():
                for copy in halo_package(b, -outer, device_at(slab + outer, b), k, 2):
                    copy.wait_send()

        for copy in halo_package(block, inner, partner, 0, 1):
            copy.wait_recv()
        for copy in local_copies(True):
            copy.wait()

    @pl.when(jnp.logical_not(same))
    def _():
        for copy in halo_package(paired, inner, partner, 0, 1):
            copy.wait_send()
        for n in range(3):
            own_package(n, block, partner).wait_recv()
        for copy in local_copies(False):
            copy.wait()

    @pl.when(there(outer, 0))
    def _():
        for copy in halo_package(block, outer, partner, 0, 2):
            copy.wait_recv()

    scaled = TIME_RATIO * courant[:, pl.ds(8, 24), :]
    courant[:, pl.ds(8, 24), :] = scaled * scaled

    order = (4, 5, 6, 7, 2, 3, 0, 1)

    def halo(slot, k, forth):
        ds, db = SIDES[k]
        opposite = SIDES.index((-ds, -db))
        if k >= 4:
            begin = corner_out.at[k - 4]
            end = corner_in.at[slot, (opposite if forth else k) - 4]
        else:
            begin = w.at[slot, pl.ds(PLANE0, 8), pl.ds(ROW0, 8), :]
            sign = -1 if forth else 1
            end = w.at[
                slot, pl.ds(PLANE0 + 8 * sign * ds, 8), pl.ds(ROW0 + 8 * sign * db, 8), :
            ]
        return pltpu.make_async_remote_copy(
            begin, end, halo_send.at[k], halo_recv.at[slot, opposite if forth else k],
            device_id=device_at(slab + ds, block + db), device_id_type=MESH_ID,
        )

    def corner_rows(k, outside):
        ds, db = SIDES[k]
        plane = (16 if ds > 0 else 4) if outside else (12 if ds > 0 else 8)
        row = (24 if db > 0 else 12) if outside else (20 if db > 0 else 16)
        return plane, row

    def stage_corner(slot, k):
        plane, row = corner_rows(k, False)
        for n in range(4):
            corner_out[k - 4, n // 2, pl.ds(4 * (n % 2), 4), :] = w[slot, plane + n, pl.ds(row, 4), :]

    def place_corner(slot, k):
        plane, row = corner_rows(k, True)
        for n in range(4):
            w[slot, plane + n, pl.ds(row, 4), :] = corner_in[slot, k - 4, n // 2, pl.ds(4 * (n % 2), 4), :]

    own = (pl.ds(PLANE0, 8), pl.ds(ROW0, 8))

    def record(values, n):
        top = jnp.broadcast_to(values[:, :, 0:1], values.shape)
        for half in range(nrec // 128):
            part = jnp.sum(top * hits[:, :, half * 128 : (half + 1) * 128], axis=0)
            row = n * (nrec // 128) + half
            record_rows[row // 8, pl.ds(lax.rem(row, 8), 1), :] = jnp.sum(part, axis=0, keepdims=True)

    def settle(slot, sides):
        for k in sides:

            @pl.when(there(*SIDES[k]))
            def _():
                halo(slot, k, False).wait_recv()
                if k >= 4:
                    place_corner(slot, k)

    def sent(slot):
        for k in order:

            @pl.when(there(*SIDES[k]))
            def _():
                halo(slot, k, True).wait_send()

    def first(slot, m, arriving):
        pulse = wavelet[2 * m]
        here = w.at[slot]
        if arriving:
            settle(slot, (0, 1, 4, 5, 6, 7))
        for p0 in (4, 16):
            new = advance(here, v, courant, mask, pulse, zmask, p0, 4, ROW0)
            v[pl.ds(p0, 4), pl.ds(ROW0, 8), :] = new
        if arriving:
            settle(slot, (2, 3))
        for p0 in range(8, 16, 2):
            for r0 in (12, 20):
                new = advance(here, v, courant, mask, pulse, zmask, p0, 2, r0)
                v[pl.ds(p0, 2), pl.ds(r0, 8), :] = new

    def second(slot, m, target):
        pulse = wavelet[2 * m + 1]
        for p0 in range(8, 16, 2):
            new = advance(v, w.at[slot], courant, mask, pulse, zmask, p0, 2, ROW0)
            target[pl.ds(p0, 2), pl.ds(ROW0, 8), :] = new

    pairs = wavelet.shape[0] // 2

    def ring(k, buffer, me, n, address, forth, d):
        other = lax.rem(me + (d if forth else n - d), n)
        return pltpu.make_async_remote_copy(
            buffer.at[me], buffer.at[me if forth else other],
            ring_send.at[k, d], ring_recv.at[k, me if forth else other],
            device_id=address(other), device_id_type=MESH_ID,
        )

    def spread(k, buffer, me, address):
        for d in range(1, buffer.shape[0]):
            ring(k, buffer, me, buffer.shape[0], address, True, d).start()

    def gathered(k, buffer, me, address):
        for d in range(1, buffer.shape[0]):
            ring(k, buffer, me, buffer.shape[0], address, True, d).wait_send()
            ring(k, buffer, me, buffer.shape[0], address, False, d).wait_recv()
        return total_of(buffer)

    def step(m, background, arriving=True):
        slot = lax.rem(m, 2)
        later = 1 - slot
        first(slot, m, arriving)
        second(slot, m, w.at[later])
        if arriving:
            sent(slot)
        for k in range(4, 8):
            stage_corner(later, k)
        for k in order:

            @pl.when(there(*SIDES[k]))
            def _():
                halo(later, k, True).start()

        record(v[own], 2 * m)
        record(w[(later, *own)], 2 * m + 1)
        background()

    def model_ways():
        for n in range(2):
            for outward in (False, True):
                yield n, outward, (more if outward else more | True)

    def gravity_share(m):
        lax.fori_loop(share_of * (m + 1), share_of * (m + 2), forward, 0)

    def background_0():
        for n, outward, really in model_ways():

            @pl.when(really)
            def _():
                model_copy(n, outward, True).start()

        gravity_share(0)

    def body(m, unused):
        step(m, lambda: gravity_share(m))
        return unused

    def background_3():
        for g in range(ngroups):
            early_z[me_z, 0, pl.ds(g, 1), :] = jnp.sum(sums[g], axis=0, keepdims=True)
        early_z[me_z, 1] = record_rows[0]
        early_z[me_z, 2] = record_rows[1]
        spread(0, early_z, me_z, on_z)

    def background_4():
        loads[1].wait()
        for n, outward, really in model_ways():

            @pl.when(really)
            def _():
                model_copy(n, outward, True).wait_send()
                model_copy(n, outward, False).wait_recv()

        lax.fori_loop(0, 8, cross_plane, 0)

    def background_5():
        early_x[me_x] = gathered(0, early_z, me_z, on_z)
        spread(1, early_x, me_x, on_x)

    def background_6():
        early_y[me_y] = gathered(1, early_x, me_x, on_x)
        spread(2, early_y, me_y, on_y)
        late_z[me_z, 0] = record_rows[2]
        late_z[me_z, 1] = record_rows[3]
        spread(3, late_z, me_z, on_z)

    def put_traces(rows_at, first_step, count):
        for n in range(count):
            for half in range(2):
                traces[pl.ds(first_step + n, 1), pl.ds(128 * half, 128)] = rows_at[
                    2 * n + half : 2 * n + half + 1, :
                ]

    step(0, background_0, False)
    lax.fori_loop(1, 3, body, 0)
    step(3, background_3)
    step(4, background_4)
    step(5, background_5)
    step(6, background_6)
    slot = (pairs - 1) % 2
    first(slot, pairs - 1, True)
    second(slot, pairs - 1, w.at[1 - slot])
    sent(slot)
    last = w.at[1 - slot]

    def handing(to, k):
        return pltpu.make_async_remote_copy(
            last.at[own], field.at[:, pl.ds(rows, 8), :],
            tail_send.at[to, k], tail_recv.at[block],
            device_id=(*device_at(slab, 2 * to + core)[:4], k), device_id_type=MESH_ID,
        )

    for to in range(blocks // 2):
        for k in range(2):

            @pl.when((2 * to + core != block) | (k != core))
            def _():
                handing(to, k).start()

    @pl.when(same)
    def _():
        field[:, pl.ds(rows, 8), :] = last[own]

    record(v[own], 2 * pairs - 2)
    record(last[own], 2 * pairs - 1)
    end_z[me_z] = record_rows[3, pl.ds(4, 4), :]
    spread(6, end_z, me_z, on_z)
    total = gathered(2, early_y, me_y, on_y)
    left_over = total[0, :ngroups] - stations[2]
    stations[0] = left_over
    residual[...] = stations[0, pl.ds(own_group, 1), :]
    for g in range(ngroups):
        spreading[pl.ds(128 * g, 128), :] = column(left_over[g : g + 1, :]).astype(jnp.bfloat16)
    put_traces(total[1], 0, 4)
    put_traces(total[2], 4, 4)
    lax.fori_loop(0, 4, adjoint, 0)
    late_x[me_x] = gathered(3, late_z, me_z, on_z)
    late_x[me_x, 1, pl.ds(4, 4), :] = gathered(6, end_z, me_z, on_z)
    spread(4, late_x, me_x, on_x)
    lax.fori_loop(4, 7, adjoint, 0)
    late_y[me_y] = gathered(4, late_x, me_x, on_x)
    spread(5, late_y, me_y, on_y)
    lax.fori_loop(7, 8, adjoint, 0)
    total = gathered(5, late_y, me_y, on_y)
    put_traces(total[0], 8, 4)
    put_traces(total[1], 12, 4)
    for to in range(blocks // 2):
        for k in range(2):

            @pl.when((2 * to + core != block) | (k != core))
            def _():
                handing(to, k).wait_send()

    for b in range(blocks):

        @pl.when((b != block) | jnp.logical_not(same))
        def _():
            pltpu.make_async_remote_copy(
                last.at[own], field.at[:, pl.ds(8 * b, 8), :],
                tail_send.at[0, 0], tail_recv.at[b],
                device_id=partner, device_id_type=MESH_ID,
            ).wait_recv()


def store_kernel(*refs):
    copies = [pltpu.make_async_copy(refs[n], refs[5 + n], refs[10].at[n]) for n in range(5)]
    for copy in copies:
        copy.start()
    for copy in copies:
        copy.wait()


def in_hbm(array):
    return pltpu.with_memory_space_constraint(array, pltpu.HBM)


def per_device(
    p_now, p_prev, velocity, density, wavelet, source_cell, receiver_cells, station_cells, observed
):
    planes, lateral, vertical = p_now.shape
    nrec = receiver_cells.shape[0]
    blocks = lax.axis_size("station_hi") * 2
    nx, nz = lax.axis_size("x"), lax.axis_size("z")
    group = station_cells.shape[0]
    f32 = jnp.float32
    padded = (24, 40, vertical)
    vmem, smem = (pl.BlockSpec(memory_space=space) for space in (pltpu.VMEM, pltpu.SMEM))
    hbm = pl.BlockSpec(memory_space=pltpu.HBM)
    dma = pltpu.SemaphoreType.DMA
    longest = max(nz, 2 * nx, blocks)
    results = pl.pallas_call(
        step_kernel,
        out_shape=(
            jax.ShapeDtypeStruct(p_now.shape, f32),
            jax.ShapeDtypeStruct((wavelet.shape[0], nrec), f32),
            jax.ShapeDtypeStruct((1, group), f32),
            jax.ShapeDtypeStruct((planes, lateral // blocks, vertical), f32),
            jax.ShapeDtypeStruct((3, *p_now.shape), f32),
        ),
        in_specs=[hbm] * 4 + [smem] * 2 + [hbm] * 3,
        out_specs=(vmem,) * 5,
        scratch_shapes=[
            pltpu.VMEM((1, nrec), jnp.int32), pltpu.VMEM((1, group), jnp.int32),
            pltpu.VMEM((1, group), f32), dma((3,)),
            pltpu.VMEM((2, *padded), f32),
            pltpu.VMEM(padded, f32),
            pltpu.VMEM(padded, f32),
            pltpu.VMEM(padded, f32),
            pltpu.VMEM((8, 8, vertical), f32),
            pltpu.VMEM((8, 8, nrec), f32),
            dma((4, 4)), dma((3, 4)), dma((8,)), dma((2, 8)), dma((blocks // 2, 2)), dma((blocks,)),
            pltpu.VMEM((blocks, 8, group), f32),
            pltpu.VMEM((3, blocks, group), f32),
            pltpu.VMEM((2, vertical, 128), f32),
            pltpu.VMEM((planes * 4, 2 * vertical, blocks * group), jnp.bfloat16),
            pltpu.VMEM((blocks, 8, group), f32),
            pltpu.VMEM((1, blocks * group), f32),
            dma((blocks,)), dma((blocks,)),
            pltpu.VMEM((2, planes + 2, lateral + 16, vertical), f32),
            dma((2, 2)), dma((2, 2)), dma((5,)),
            pltpu.VMEM((4, 8, 128), f32),
            *(pltpu.VMEM((n, 3, 8, 128), f32) for n in (nz, 2 * nx, blocks)),
            *(pltpu.VMEM((n, 2, 8, 128), f32) for n in (nz, 2 * nx, blocks)),
            pltpu.VMEM((nz, 4, 128), f32),
            dma((7, longest)), dma((7, longest)),
            pltpu.VMEM((4, 2, 8, vertical), f32),
            pltpu.VMEM((2, 4, 2, 8, vertical), f32),
            pltpu.VMEM((blocks * group, 128), jnp.bfloat16),
        ],
        compiler_params=pltpu.CompilerParams(
            collective_id=0, has_side_effects=True, vmem_limit_bytes=48 * 2**20
        ),
    )(
        *map(in_hbm, (p_now, p_prev, velocity, density)), wavelet, source_cell,
        *(in_hbm(a.reshape(1, -1)) for a in (receiver_cells, station_cells, observed)),
    )
    field, traces, residual, gradient, crossed = pl.pallas_call(
        store_kernel,
        out_shape=tuple(jax.ShapeDtypeStruct(r.shape, r.dtype) for r in results),
        in_specs=[vmem] * 5,
        out_specs=(hbm,) * 5,
        scratch_shapes=[dma((5,))],
        compiler_params=pltpu.CompilerParams(vmem_limit_bytes=2 * 2**20),
    )(*results)
    return field, traces, residual.reshape(-1), gradient, crossed


def solution(mesh):
    split = Mesh(mesh.devices.reshape(*SPLIT, mesh.shape["station"] // 2, 2), MESH)
    slabs = P(MP, None, None)
    return jax.shard_map(
        per_device,
        mesh=split,
        in_specs=(slabs, slabs, slabs, slabs, P(), P(), P(), P(STATION), P(STATION)),
        out_specs=(slabs, P(), P(STATION), P(MP, STATION, None), P(None, MP, None, None)),
        check_vma=False,
    )
```

```python
import jax
import jax.numpy as jnp
from jax import lax
from jax.experimental import pallas as pl
from jax.experimental.pallas import tpu as pltpu
from jax.sharding import Mesh
from jax.sharding import PartitionSpec as P

MP = ("x", "z", "y_lo")
STATION = ("station_hi", "core")
MESH = MP + STATION
SPLIT = (4, 12, 2)
STENCIL = (-205.0 / 72.0, 8.0 / 5.0, -1.0 / 5.0, 8.0 / 315.0, -1.0 / 560.0)
TIME_RATIO = 0.1
MESH_ID = pl.DeviceIdType.MESH
SIDES = ((-1, 0), (1, 0), (0, -1), (0, 1), (-1, -1), (-1, 1), (1, -1), (1, 1))
ROW0 = 16
PLANE0 = 8


def place():
    x, z, low, high, core = (lax.axis_index(axis) for axis in MESH)
    nz = lax.axis_size("z")
    slab = (x * nz + z) * 2 + core
    return slab, high * 2 + low, low, core


def device_at(slab, block):
    nz = lax.axis_size("z")
    column = slab // 2
    return (column // nz, lax.rem(column, nz), lax.rem(block, 2), block // 2, lax.rem(slab, 2))


def advance(ref, prev, courant, mask, pulse, zmask, p0, planes, r0):
    rows = pl.ds(r0, 8)
    here = ref[pl.ds(p0, planes), rows, :]
    lap = 3.0 * STENCIL[0] * here
    for d in range(1, 5):
        pairs = ref[pl.ds(p0 + d, planes), rows, :] + ref[pl.ds(p0 - d, planes), rows, :]
        pairs = pairs + ref[pl.ds(p0, planes), pl.ds(r0 + d, 8), :]
        pairs = pairs + ref[pl.ds(p0, planes), pl.ds(r0 - d, 8), :]
        lap = lap + STENCIL[d] * pairs
        lap = lap + pltpu.roll(here, d, 2) * zmask[2 * d - 2][None]
        lap = lap + pltpu.roll(here, here.shape[2] - d, 2) * zmask[2 * d - 1][None]
    at = (pl.ds(p0, planes), rows)
    return 2.0 * here - prev[at] + courant[at] * lap + pulse * mask[at]


def total_of(parts):
    total = parts[0]
    for k in range(1, parts.shape[0]):
        total = total + parts[k]
    return total


def step_kernel(
    p_now, p_prev, velocity, density, wavelet, source, receivers_in, cells_in, observed_in,
    field, traces, residual, gradient, crossed,
    receivers, cells, observed, small,
    w, v, courant, mask, zmask, hits,
    init_send, init_recv, halo_send, halo_recv, tail_send, tail_recv,
    groups, stations, depth, tiles, sums, low_row, group_send, group_recv,
    models, model_send, model_recv, local,
    record_rows, early_z, early_x, early_y, late_z, late_x, late_y, end_z,
    ring_send, ring_recv, corner_out, corner_in, spreading,
):
    slab, block, low, core = place()
    slabs = lax.axis_size(MP)
    blocks = lax.axis_size("station_hi") * 2
    lateral, vertical = p_now.shape[1:]
    same = core == low
    inner = 1 - 2 * core
    outer = -inner
    pair = 1 - 2 * low

    def there(ds, db):
        return (slab + ds >= 0) & (slab + ds < slabs) & (block + db >= 0) & (block + db < blocks)

    def window(b):
        start = jnp.clip(8 * (b - 1), 0, lateral - 24)
        return pl.multiple_of(start, 8), pl.multiple_of(ROW0 + start - 8 * b, 8)

    barrier = pltpu.get_barrier_semaphore()
    for other in range(2 * blocks):
        b, k = other // 2, other % 2

        @pl.when((b != block) | (k != core))
        def _():
            pl.semaphore_signal(
                barrier, 1, device_id=device_at(slab - core + k, b), device_id_type=MESH_ID
            )

    for db in (-1, 0, 1):

        @pl.when(there(outer, db))
        def _():
            pl.semaphore_signal(
                barrier, 1, device_id=device_at(slab + outer, block + db), device_id_type=MESH_ID
            )

    x, z, high = lax.axis_index("x"), lax.axis_index("z"), block // 2
    nx, nz = lax.axis_size("x"), lax.axis_size("z")

    def on_z(k):
        return (x, k, low, high, core)

    def on_x(k):
        return (k // 2, z, low, high, lax.rem(k, 2))

    def on_y(k):
        return device_at(slab, k)

    me_z, me_x, me_y = z, 2 * x + core, block
    for d in range(1, nz):
        pl.semaphore_signal(
            barrier, 1, device_id=on_z(lax.rem(z + d, nz)), device_id_type=MESH_ID
        )
    for d in range(1, nx):
        for k in range(2):
            pl.semaphore_signal(
                barrier, 1, device_id=on_x(2 * lax.rem(x + d, nx) + k), device_id_type=MESH_ID
            )
    kept = (x * nz + z) * 2 + low
    onward = 2 * low - 1
    beyond = kept + onward
    more = (beyond >= 0) & (beyond < slabs)
    far = (beyond // (2 * nz), lax.rem(beyond // 2, nz), 1 - low, high, core)

    @pl.when(more)
    def _():
        pl.semaphore_signal(barrier, 1, device_id=far, device_id_type=MESH_ID)

    smalls = [
        pltpu.make_async_copy(a, b, small.at[n])
        for n, (a, b) in enumerate(
            (
                (cells_in, cells), (observed_in, observed), (receivers_in, receivers),
            )
        )
    ]
    for copy in smalls:
        copy.start()

    start, to = window(block)
    rows = pl.multiple_of(8 * block, 8)
    inside = (pl.ds(1, 8), pl.ds(8, lateral))
    loads = [
        pltpu.make_async_copy(density, models.at[(1, *inside)], local.at[3]),
        pltpu.make_async_copy(velocity, models.at[(0, *inside)], local.at[4]),
    ]
    for copy in loads:
        copy.start()
    inner_left = inner < 0

    def local_copies(own_slab):
        if own_slab:
            pairs_of = [
                (a.at[:, pl.ds(start, 24), :], p.at[pl.ds(PLANE0, 8), pl.ds(to, 24), :])
                for a, p in ((p_now, w.at[0]), (p_prev, v), (velocity, courant))
            ]
        else:
            pairs_of = [
                (
                    p_now.at[:, pl.ds(start, 24), :],
                    w.at[0, pl.ds(jnp.where(inner_left, 0, 16), 8), pl.ds(to, 24), :],
                )
            ] + [
                (
                    a.at[pl.ds(jnp.where(inner_left, 4, 0), 4), pl.ds(rows, 8), :],
                    p.at[pl.ds(jnp.where(inner_left, 4, 16), 4), pl.ds(ROW0, 8), :],
                )
                for a, p in ((p_prev, v), (velocity, courant))
            ]
        return [
            pltpu.make_async_copy(a, b, local.at[n]) for n, (a, b) in enumerate(pairs_of)
        ]

    @pl.when(same)
    def _():
        for copy in local_copies(True):
            copy.start()

    @pl.when(jnp.logical_not(same))
    def _():
        for copy in local_copies(False):
            copy.start()

    def clear(at):
        shape = (at[0].size, at[1].size, vertical)
        for ref in (w.at[0], w.at[1], v, courant):
            ref[at] = jnp.zeros(shape, jnp.float32)

    pl.when(slab == 0)(lambda: clear((pl.ds(0, 8), pl.ds(8, 24))))
    pl.when(slab == slabs - 1)(lambda: clear((pl.ds(16, 8), pl.ds(8, 24))))
    pl.when(block == 0)(lambda: clear((pl.ds(0, 24), pl.ds(8, 8))))
    pl.when(block == blocks - 1)(lambda: clear((pl.ds(0, 24), pl.ds(24, 8))))
    for n in range(2):
        for plane in (0, 9):

            @pl.when(kept == (0 if plane == 0 else slabs - 1))
            def _():
                models[n, plane, pl.ds(8, lateral), :] = jnp.zeros((lateral, vertical), jnp.float32)

        for row in (0, 8 + lateral):
            models[n, :, pl.ds(row, 8), :] = jnp.zeros((10, 8, vertical), jnp.float32)

    crossing = sum(jnp.where(there(outer, db), 1, 0) for db in (-1, 0, 1))
    pl.semaphore_wait(
        barrier, 2 * blocks - 1 + crossing + nz - 1 + 2 * (nx - 1) + jnp.where(more, 1, 0)
    )

    own_group = 2 * high + core
    smalls[0].wait()
    smalls[1].wait()
    sizes = (lateral.bit_length() - 1, lateral - 1)
    groups[own_group, pl.ds(0, 1), :] = (cells[...] >> sizes[0]).astype(jnp.float32)
    groups[own_group, pl.ds(1, 1), :] = (cells[...] & sizes[1]).astype(jnp.float32)
    groups[own_group, pl.ds(2, 1), :] = observed[...]

    def group_copy(d, forth):
        other = lax.rem(own_group + (d if forth else blocks - d), blocks)
        return pltpu.make_async_remote_copy(
            groups.at[own_group], groups.at[own_group if forth else other],
            group_send.at[d], group_recv.at[own_group if forth else other],
            device_id=(x, z, low, other // 2, lax.rem(other, 2)), device_id_type=MESH_ID,
        )

    for d in range(1, blocks):
        group_copy(d, True).start()

    arrays = (p_now, p_prev, velocity)
    places = (w.at[0], v, courant)

    def own_package(n, b, target):
        begin, landing = window(b)
        return pltpu.make_async_remote_copy(
            arrays[n].at[:, pl.ds(begin, 24), :],
            places[n].at[pl.ds(PLANE0, 8), pl.ds(landing, 24), :],
            init_send.at[3, n], init_recv.at[0, n], device_id=target, device_id_type=MESH_ID,
        )

    def halo_package(b, side, target, k, landing):
        begin, to_row = window(b)
        left = side < 0
        near, far_off = jnp.where(left, 4, 0), jnp.where(left, 0, 4)
        near_to, far_to = jnp.where(left, 4, 16), jnp.where(left, 0, 20)
        home = pl.multiple_of(8 * b, 8)
        block_at, block_to = pl.ds(home, 8), pl.ds(ROW0, 8)
        parts = [
            (p_now.at[pl.ds(near, 4), pl.ds(begin, 24), :], w.at[0, pl.ds(near_to, 4), pl.ds(to_row, 24), :]),
            (p_now.at[pl.ds(far_off, 4), block_at, :], w.at[0, pl.ds(far_to, 4), block_to, :]),
        ] + [
            (a.at[pl.ds(near, 4), block_at, :], p.at[pl.ds(near_to, 4), block_to, :])
            for a, p in ((p_prev, v), (velocity, courant))
        ]
        return [
            pltpu.make_async_remote_copy(
                a, p, init_send.at[k, n], init_recv.at[landing, n],
                device_id=target, device_id_type=MESH_ID,
            )
            for n, (a, p) in enumerate(parts)
        ]

    paired = block + pair
    across = lax.rem(block - pair + blocks, blocks)
    partner = device_at(slab, paired)

    @pl.when(same)
    def _():
        own_package(0, paired, partner).start()
        for n in (1, 2):
            own_package(n, across, device_at(slab, across)).start()
        for k, b in ((1, block), (2, paired)):

            @pl.when(there(outer, 0))
            def _():
                for copy in halo_package(b, -outer, device_at(slab + outer, b), k, 2):
                    copy.start()

    @pl.when(jnp.logical_not(same))
    def _():
        for copy in halo_package(paired, inner, partner, 0, 1):
            copy.start()

    def model_copy(n, outward, forth):
        e = onward if outward else -onward
        if forth:
            plane, landing = jnp.where(e > 0, 7, 0), jnp.where(e > 0, 0, 9)
        else:
            plane, landing = 0, jnp.where(e > 0, 9, 0)
        k = 1 if outward else 0
        return pltpu.make_async_remote_copy(
            (velocity, density)[n].at[plane], models.at[n, landing, pl.ds(8, lateral), :],
            model_send.at[n, k], model_recv.at[n, k],
            device_id=far if outward else partner, device_id_type=MESH_ID,
        )

    for copy in smalls[2:]:
        copy.wait()
    source_cell = source[0]
    source_z = lax.rem(source_cell, vertical)
    source_xy = source_cell // vertical
    source_y = lax.rem(source_xy, lateral)
    source_x = source_xy // lateral
    shape = (24, 24, vertical)
    at_x = lax.broadcasted_iota(jnp.int32, shape, 0) + (8 * slab - PLANE0)
    at_y = lax.broadcasted_iota(jnp.int32, shape, 1) + (8 * block + 8 - ROW0)
    at_z = lax.broadcasted_iota(jnp.int32, shape, 2)
    hit = (at_x == source_x) & (at_y == source_y) & (at_z == source_z)
    mask[:, pl.ds(8, 24), :] = jnp.where(hit, 1.0, 0.0)
    lane = lax.broadcasted_iota(jnp.int32, (8, vertical), 1)
    for d in range(1, 5):
        zmask[2 * d - 2] = jnp.where(lane >= d, STENCIL[d], 0.0)
        zmask[2 * d - 1] = jnp.where(lane < vertical - d, STENCIL[d], 0.0)
    nrec = receivers.shape[1]
    cell = (8 * slab + lax.broadcasted_iota(jnp.int32, (8, 8, nrec), 0)) * lateral + (
        8 * block + lax.broadcasted_iota(jnp.int32, (8, 8, nrec), 1)
    )
    hits[...] = jnp.where(cell == receivers[...][None], 1.0, 0.0)

    step_z = lax.broadcasted_iota(jnp.int32, (vertical, 128), 0).astype(jnp.float32) + 1.0
    depth[0] = step_z
    depth[1] = step_z * step_z
    share = pl.multiple_of(8 * own_group, 8)
    ngroups = groups.shape[0]
    sums[...] = jnp.zeros(sums.shape, jnp.float32)
    record_rows[3] = jnp.zeros((8, 128), jnp.float32)
    eye = lax.broadcasted_iota(jnp.int32, (128, 128), 0) == lax.broadcasted_iota(
        jnp.int32, (128, 128), 1
    )

    def column(row):
        picked = jnp.where(eye, jnp.broadcast_to(row, (128, 128)), 0.0).astype(jnp.bfloat16)
        ones = jnp.ones((128, 128), jnp.bfloat16)
        return jnp.dot(picked, ones, preferred_element_type=jnp.float32)

    def forward(q, unused):
        p, r = q // 4, 2 * lax.rem(q, 4)
        dx = (8 * kept + p).astype(jnp.float32) - stations[0]
        for u in range(2):
            dy = (share + r + u).astype(jnp.float32) - stations[1]
            flat = dx * dx + dy * dy
            weight = column(models[1, p + 1, pl.ds(8 + share + r + u, 1), :])
            for g in range(ngroups):
                inverse = lax.rsqrt(flat[g : g + 1, :] + depth[1])
                tile = ((depth[0] * inverse) * (inverse * inverse)).astype(jnp.bfloat16)
                tiles[q, pl.ds(u * vertical, vertical), pl.ds(g * 128, 128)] = tile
                part = tile.astype(jnp.float32) * weight
                sums[g] += jnp.sum(part.reshape(vertical // 8, 8, 128), axis=0)
        return unused

    def adjoint(p, unused):
        each = tiles.shape[0] // 8
        slab_tiles = tiles[pl.ds(p * each, each)].reshape(each * 2 * vertical, ngroups * 128)
        out = jnp.dot(slab_tiles, spreading[...], preferred_element_type=jnp.float32)
        for r in range(2 * each):
            unit = jnp.where(eye, out[vertical * r : vertical * (r + 1)], 0.0)
            part = jnp.sum(unit.reshape(vertical // 8, 8, 128), axis=0)
            gradient[p, pl.ds(r, 1), :] = jnp.sum(part, axis=0, keepdims=True)
        return unused

    def cross_plane(p, unused):
        lanes = lax.broadcasted_iota(jnp.int32, (lateral, vertical), 1)

        def slopes(f):
            mid = f[p + 1, pl.ds(8, lateral), :]
            along_x = (f[p + 2, pl.ds(8, lateral), :] - f[p, pl.ds(8, lateral), :]) * 0.5
            along_y = (f[p + 1, pl.ds(9, lateral), :] - f[p + 1, pl.ds(7, lateral), :]) * 0.5
            after = jnp.where(lanes < vertical - 1, pltpu.roll(mid, vertical - 1, 1), 0.0)
            before = jnp.where(lanes > 0, pltpu.roll(mid, 1, 1), 0.0)
            return along_x, along_y, (after - before) * 0.5

        vx, vy, vz = slopes(models.at[0])
        qx, qy, qz = slopes(models.at[1])
        crossed[0, p] = vy * qz - vz * qy
        crossed[1, p] = vz * qx - vx * qz
        crossed[2, p] = vx * qy - vy * qx
        return unused

    loads[0].wait()
    for d in range(1, blocks):
        group_copy(d, True).wait_send()
        group_copy(d, False).wait_recv()
    for g in range(ngroups):
        for n in range(3):
            stations[n, pl.ds(g, 1), :] = groups[g, pl.ds(n, 1), :]
    pairs_all = tiles.shape[0]
    at_first, share_of = pairs_all // 8, pairs_all * 3 // 16
    lax.fori_loop(0, at_first, forward, 0)

    @pl.when(same)
    def _():
        own_package(0, paired, partner).wait_send()
        for n in (1, 2):
            own_package(n, across, device_at(slab, across)).wait_send()
        for k, b in ((1, block), (2, paired)):

            @pl.when(there(outer, 0))
            def _():
                for copy in halo_package(b, -outer, device_at(slab + outer, b), k, 2):
                    copy.wait_send()

        for copy in halo_package(block, inner, partner, 0, 1):
            copy.wait_recv()
        for copy in local_copies(True):
            copy.wait()

    @pl.when(jnp.logical_not(same))
    def _():
        for copy in halo_package(paired, inner, partner, 0, 1):
            copy.wait_send()
        for n in range(3):
            own_package(n, block, partner).wait_recv()
        for copy in local_copies(False):
            copy.wait()

    @pl.when(there(outer, 0))
    def _():
        for copy in halo_package(block, outer, partner, 0, 2):
            copy.wait_recv()

    scaled = TIME_RATIO * courant[:, pl.ds(8, 24), :]
    courant[:, pl.ds(8, 24), :] = scaled * scaled

    order = (4, 5, 6, 7, 2, 3, 0, 1)

    def halo(slot, k, forth):
        ds, db = SIDES[k]
        opposite = SIDES.index((-ds, -db))
        if k >= 4:
            begin = corner_out.at[k - 4]
            end = corner_in.at[slot, (opposite if forth else k) - 4]
        else:
            begin = w.at[slot, pl.ds(PLANE0, 8), pl.ds(ROW0, 8), :]
            sign = -1 if forth else 1
            end = w.at[
                slot, pl.ds(PLANE0 + 8 * sign * ds, 8), pl.ds(ROW0 + 8 * sign * db, 8), :
            ]
        return pltpu.make_async_remote_copy(
            begin, end, halo_send.at[k], halo_recv.at[slot, opposite if forth else k],
            device_id=device_at(slab + ds, block + db), device_id_type=MESH_ID,
        )

    def corner_rows(k, outside):
        ds, db = SIDES[k]
        plane = (16 if ds > 0 else 4) if outside else (12 if ds > 0 else 8)
        row = (24 if db > 0 else 12) if outside else (20 if db > 0 else 16)
        return plane, row

    def stage_corner(slot, k):
        plane, row = corner_rows(k, False)
        for n in range(4):
            corner_out[k - 4, n // 2, pl.ds(4 * (n % 2), 4), :] = w[slot, plane + n, pl.ds(row, 4), :]

    def place_corner(slot, k):
        plane, row = corner_rows(k, True)
        for n in range(4):
            w[slot, plane + n, pl.ds(row, 4), :] = corner_in[slot, k - 4, n // 2, pl.ds(4 * (n % 2), 4), :]

    own = (pl.ds(PLANE0, 8), pl.ds(ROW0, 8))

    def record(values, n):
        top = jnp.broadcast_to(values[:, :, 0:1], values.shape)
        for half in range(nrec // 128):
            part = jnp.sum(top * hits[:, :, half * 128 : (half + 1) * 128], axis=0)
            row = n * (nrec // 128) + half
            record_rows[row // 8, pl.ds(lax.rem(row, 8), 1), :] = jnp.sum(part, axis=0, keepdims=True)

    def settle(slot, sides):
        for k in sides:

            @pl.when(there(*SIDES[k]))
            def _():
                halo(slot, k, False).wait_recv()
                if k >= 4:
                    place_corner(slot, k)

    def sent(slot):
        for k in order:

            @pl.when(there(*SIDES[k]))
            def _():
                halo(slot, k, True).wait_send()

    def first(slot, m, arriving):
        pulse = wavelet[2 * m]
        here = w.at[slot]
        if arriving:
            settle(slot, (0, 1, 4, 5, 6, 7))
        for p0 in (4, 16):
            new = advance(here, v, courant, mask, pulse, zmask, p0, 4, ROW0)
            v[pl.ds(p0, 4), pl.ds(ROW0, 8), :] = new
        if arriving:
            settle(slot, (2, 3))
        for p0 in range(8, 16, 2):
            for r0 in (12, 20):
                new = advance(here, v, courant, mask, pulse, zmask, p0, 2, r0)
                v[pl.ds(p0, 2), pl.ds(r0, 8), :] = new

    def second(slot, m, target):
        pulse = wavelet[2 * m + 1]
        for p0 in range(8, 16, 2):
            new = advance(v, w.at[slot], courant, mask, pulse, zmask, p0, 2, ROW0)
            target[pl.ds(p0, 2), pl.ds(ROW0, 8), :] = new

    pairs = wavelet.shape[0] // 2

    def ring(k, buffer, me, n, address, forth, d):
        other = lax.rem(me + (d if forth else n - d), n)
        return pltpu.make_async_remote_copy(
            buffer.at[me], buffer.at[me if forth else other],
            ring_send.at[k, d], ring_recv.at[k, me if forth else other],
            device_id=address(other), device_id_type=MESH_ID,
        )

    def spread(k, buffer, me, address):
        for d in range(1, buffer.shape[0]):
            ring(k, buffer, me, buffer.shape[0], address, True, d).start()

    def gathered(k, buffer, me, address):
        for d in range(1, buffer.shape[0]):
            ring(k, buffer, me, buffer.shape[0], address, True, d).wait_send()
            ring(k, buffer, me, buffer.shape[0], address, False, d).wait_recv()
        return total_of(buffer)

    def step(m, background, arriving=True):
        slot = lax.rem(m, 2)
        later = 1 - slot
        first(slot, m, arriving)
        second(slot, m, w.at[later])
        if arriving:
            sent(slot)
        for k in range(4, 8):
            stage_corner(later, k)
        for k in order:

            @pl.when(there(*SIDES[k]))
            def _():
                halo(later, k, True).start()

        record(v[own], 2 * m)
        record(w[(later, *own)], 2 * m + 1)
        background()

    def model_ways():
        for n in range(2):
            for outward in (False, True):
                yield n, outward, (more if outward else more | True)

    def gravity_share(m):
        lax.fori_loop(at_first + share_of * m, at_first + share_of * (m + 1), forward, 0)

    def background_0():
        for n, outward, really in model_ways():

            @pl.when(really)
            def _():
                model_copy(n, outward, True).start()

        gravity_share(0)

    def body(m, unused):
        step(m, lambda: gravity_share(m))
        return unused

    def background_4():
        lax.fori_loop(at_first + share_of * 4, pairs_all, forward, 0)
        for g in range(ngroups):
            early_z[me_z, 0, pl.ds(g, 1), :] = jnp.sum(sums[g], axis=0, keepdims=True)
        early_z[me_z, 1] = record_rows[0]
        early_z[me_z, 2] = record_rows[1]
        spread(0, early_z, me_z, on_z)

    def background_5():
        loads[1].wait()
        for n, outward, really in model_ways():

            @pl.when(really)
            def _():
                model_copy(n, outward, True).wait_send()
                model_copy(n, outward, False).wait_recv()

        lax.fori_loop(0, 8, cross_plane, 0)

    def background_6():
        early_x[me_x] = gathered(0, early_z, me_z, on_z)
        spread(1, early_x, me_x, on_x)
        late_z[me_z, 0] = record_rows[2]
        late_z[me_z, 1] = record_rows[3]
        spread(3, late_z, me_z, on_z)

    def put_traces(rows_at, first_step, count):
        for n in range(count):
            for half in range(2):
                traces[pl.ds(first_step + n, 1), pl.ds(128 * half, 128)] = rows_at[
                    2 * n + half : 2 * n + half + 1, :
                ]

    step(0, background_0, False)
    lax.fori_loop(1, 4, body, 0)
    step(4, background_4)
    step(5, background_5)
    step(6, background_6)
    slot = (pairs - 1) % 2
    first(slot, pairs - 1, True)
    second(slot, pairs - 1, w.at[1 - slot])
    sent(slot)
    last = w.at[1 - slot]

    def handing(to, k):
        return pltpu.make_async_remote_copy(
            last.at[own], field.at[:, pl.ds(rows, 8), :],
            tail_send.at[to, k], tail_recv.at[block],
            device_id=(*device_at(slab, 2 * to + core)[:4], k), device_id_type=MESH_ID,
        )

    record(v[own], 2 * pairs - 2)
    record(last[own], 2 * pairs - 1)
    end_z[me_z] = record_rows[3, pl.ds(4, 4), :]
    spread(6, end_z, me_z, on_z)
    early_y[me_y] = gathered(1, early_x, me_x, on_x)
    spread(2, early_y, me_y, on_y)
    for to in range(blocks // 2):
        for k in range(2):

            @pl.when((2 * to + core != block) | (k != core))
            def _():
                handing(to, k).start()

    @pl.when(same)
    def _():
        field[:, pl.ds(rows, 8), :] = last[own]

    total = gathered(2, early_y, me_y, on_y)
    left_over = total[0, :ngroups] - stations[2]
    stations[0] = left_over
    residual[...] = stations[0, pl.ds(own_group, 1), :]
    for g in range(ngroups):
        spreading[pl.ds(128 * g, 128), :] = column(left_over[g : g + 1, :]).astype(jnp.bfloat16)
    put_traces(total[1], 0, 4)
    put_traces(total[2], 4, 4)
    late_x[me_x] = gathered(3, late_z, me_z, on_z)
    late_x[me_x, 1, pl.ds(4, 4), :] = gathered(6, end_z, me_z, on_z)
    spread(4, late_x, me_x, on_x)
    lax.fori_loop(0, 4, adjoint, 0)
    late_y[me_y] = gathered(4, late_x, me_x, on_x)
    spread(5, late_y, me_y, on_y)
    lax.fori_loop(4, 8, adjoint, 0)
    total = gathered(5, late_y, me_y, on_y)
    put_traces(total[0], 8, 4)
    put_traces(total[1], 12, 4)
    for to in range(blocks // 2):
        for k in range(2):

            @pl.when((2 * to + core != block) | (k != core))
            def _():
                handing(to, k).wait_send()

    for b in range(blocks):

        @pl.when((b != block) | jnp.logical_not(same))
        def _():
            pltpu.make_async_remote_copy(
                last.at[own], field.at[:, pl.ds(8 * b, 8), :],
                tail_send.at[0, 0], tail_recv.at[b],
                device_id=partner, device_id_type=MESH_ID,
            ).wait_recv()


def store_kernel(*refs):
    copies = [pltpu.make_async_copy(refs[n], refs[5 + n], refs[10].at[n]) for n in range(5)]
    for copy in copies:
        copy.start()
    for copy in copies:
        copy.wait()


def in_hbm(array):
    return pltpu.with_memory_space_constraint(array, pltpu.HBM)


def per_device(
    p_now, p_prev, velocity, density, wavelet, source_cell, receiver_cells, station_cells, observed
):
    planes, lateral, vertical = p_now.shape
    nrec = receiver_cells.shape[0]
    blocks = lax.axis_size("station_hi") * 2
    nx, nz = lax.axis_size("x"), lax.axis_size("z")
    group = station_cells.shape[0]
    f32 = jnp.float32
    padded = (24, 40, vertical)
    vmem, smem = (pl.BlockSpec(memory_space=space) for space in (pltpu.VMEM, pltpu.SMEM))
    hbm = pl.BlockSpec(memory_space=pltpu.HBM)
    dma = pltpu.SemaphoreType.DMA
    longest = max(nz, 2 * nx, blocks)
    results = pl.pallas_call(
        step_kernel,
        out_shape=(
            jax.ShapeDtypeStruct(p_now.shape, f32),
            jax.ShapeDtypeStruct((wavelet.shape[0], nrec), f32),
            jax.ShapeDtypeStruct((1, group), f32),
            jax.ShapeDtypeStruct((planes, lateral // blocks, vertical), f32),
            jax.ShapeDtypeStruct((3, *p_now.shape), f32),
        ),
        in_specs=[hbm] * 4 + [smem] * 2 + [hbm] * 3,
        out_specs=(vmem,) * 5,
        scratch_shapes=[
            pltpu.VMEM((1, nrec), jnp.int32), pltpu.VMEM((1, group), jnp.int32),
            pltpu.VMEM((1, group), f32), dma((3,)),
            pltpu.VMEM((2, *padded), f32),
            pltpu.VMEM(padded, f32),
            pltpu.VMEM(padded, f32),
            pltpu.VMEM(padded, f32),
            pltpu.VMEM((8, 8, vertical), f32),
            pltpu.VMEM((8, 8, nrec), f32),
            dma((4, 4)), dma((3, 4)), dma((8,)), dma((2, 8)), dma((blocks // 2, 2)), dma((blocks,)),
            pltpu.VMEM((blocks, 8, group), f32),
            pltpu.VMEM((3, blocks, group), f32),
            pltpu.VMEM((2, vertical, 128), f32),
            pltpu.VMEM((planes * 4, 2 * vertical, blocks * group), jnp.bfloat16),
            pltpu.VMEM((blocks, 8, group), f32),
            pltpu.VMEM((1, blocks * group), f32),
            dma((blocks,)), dma((blocks,)),
            pltpu.VMEM((2, planes + 2, lateral + 16, vertical), f32),
            dma((2, 2)), dma((2, 2)), dma((5,)),
            pltpu.VMEM((4, 8, 128), f32),
            *(pltpu.VMEM((n, 3, 8, 128), f32) for n in (nz, 2 * nx, blocks)),
            *(pltpu.VMEM((n, 2, 8, 128), f32) for n in (nz, 2 * nx, blocks)),
            pltpu.VMEM((nz, 4, 128), f32),
            dma((7, longest)), dma((7, longest)),
            pltpu.VMEM((4, 2, 8, vertical), f32),
            pltpu.VMEM((2, 4, 2, 8, vertical), f32),
            pltpu.VMEM((blocks * group, 128), jnp.bfloat16),
        ],
        compiler_params=pltpu.CompilerParams(
            collective_id=0, has_side_effects=True, vmem_limit_bytes=48 * 2**20
        ),
    )(
        *map(in_hbm, (p_now, p_prev, velocity, density)), wavelet, source_cell,
        *(in_hbm(a.reshape(1, -1)) for a in (receiver_cells, station_cells, observed)),
    )
    field, traces, residual, gradient, crossed = pl.pallas_call(
        store_kernel,
        out_shape=tuple(jax.ShapeDtypeStruct(r.shape, r.dtype) for r in results),
        in_specs=[vmem] * 5,
        out_specs=(hbm,) * 5,
        scratch_shapes=[dma((5,))],
        compiler_params=pltpu.CompilerParams(vmem_limit_bytes=2 * 2**20),
    )(*results)
    return field, traces, residual.reshape(-1), gradient, crossed


def solution(mesh):
    split = Mesh(mesh.devices.reshape(*SPLIT, mesh.shape["station"] // 2, 2), MESH)
    slabs = P(MP, None, None)
    return jax.shard_map(
        per_device,
        mesh=split,
        in_specs=(slabs, slabs, slabs, slabs, P(), P(), P(), P(STATION), P(STATION)),
        out_specs=(slabs, P(), P(STATION), P(MP, STATION, None), P(None, MP, None, None)),
        check_vma=False,
    )
```
